32 devices in a mesh: dp: 16 (over z, x, core), seq: 2 (over y).
Axes of the slice: x: 2, y: 2, z: 4, core: 2. Of those that a mesh axis runs over, the one named last changes fastest.
Arguments:
- text_input: bfloat16 [32, 100, 768], P(('dp', 'seq')), may hold values from -6 to 6
- image_input: bfloat16 [32, 36, 1024], P(('dp', 'seq')), may hold values from -6 to 6
- caption_lengths: int32 [32], P('dp'), may hold values from 1 to 100, as said below
- text_cotangent: bfloat16 [32, 100, 768], P(('dp', 'seq')), may hold values from -6 to 6
- image_cotangent: bfloat16 [32, 36, 1024], P(('dp', 'seq')), may hold values from -6 to 6
- cross_text_proj: bfloat16 [3, 768, 1024], P(None, ('dp', 'seq')), may hold values from -0.21875 to 0.21875
- cross_image_proj: bfloat16 [3, 1024, 1024], P(None, ('dp', 'seq')), may hold values from -0.1875 to 0.1875
- cross_text_out: bfloat16 [1024, 768], P(('dp', 'seq')), may hold values from -0.4375 to 0.4375
- cross_image_out: bfloat16 [1024, 1024], P(('dp', 'seq')), may hold values from -0.5 to 0.5
- cross_text_up: bfloat16 [768, 3072], P(('dp', 'seq')), may hold values from -0.21875 to 0.21875
- cross_text_down: bfloat16 [3072, 768], P(('dp', 'seq')), may hold values from -0.109375 to 0.109375
- cross_image_up: bfloat16 [1024, 1024], P(('dp', 'seq')), may hold values from -0.1875 to 0.1875
- cross_image_down: bfloat16 [1024, 1024], P(('dp', 'seq')), may hold values from -0.1875 to 0.1875
- self_text_proj: bfloat16 [3, 768, 768], P(None, ('dp', 'seq')), may hold values from -0.21875 to 0.21875
- self_text_out: bfloat16 [768, 768], P(('dp', 'seq')), may hold values from -0.5 to 0.5
- self_text_up: bfloat16 [768, 3072], P(('dp', 'seq')), may hold values from -0.21875 to 0.21875
- self_text_down: bfloat16 [3072, 768], P(('dp', 'seq')), may hold values from -0.109375 to 0.109375
- self_image_proj: bfloat16 [3, 1024, 1024], P(None, ('dp', 'seq')), may hold values from -0.1875 to 0.1875
- self_image_out: bfloat16 [1024, 1024], P(('dp', 'seq')), may hold values from -0.4375 to 0.4375
- self_image_up: bfloat16 [1024, 1024], P(('dp', 'seq')), may hold values from -0.1875 to 0.1875
- self_image_down: bfloat16 [1024, 1024], P(('dp', 'seq')), may hold values from -0.1875 to 0.1875
- text_gains: float32 [4, 768], replicated, may hold values from 0.5 to 1.5
- image_gains: float32 [4, 1024], replicated, may hold values from 0.5 to 1.5
Outputs:
- text_output: bfloat16 [32, 100, 768], P(('dp', 'seq'))
- image_output: bfloat16 [32, 36, 1024], P(('dp', 'seq'))
- text_input_grad: float32 [32, 100, 768], P(('dp', 'seq'))
- image_input_grad: float32 [32, 36, 1024], P(('dp', 'seq'))
- cross_text_proj_grad: float32 [3, 768, 1024], P(None, None, ('dp', 'seq'))
- cross_image_proj_grad: float32 [3, 1024, 1024], P(None, None, ('dp', 'seq'))
- cross_text_out_grad: float32 [1024, 768], P(('dp', 'seq'))
- cross_image_out_grad: float32 [1024, 1024], P(('dp', 'seq'))
- cross_text_up_grad: float32 [768, 3072], P(None, ('dp', 'seq'))
- cross_text_down_grad: float32 [3072, 768], P(('dp', 'seq'))
- cross_image_up_grad: float32 [1024, 1024], P(None, ('dp', 'seq'))
- cross_image_down_grad: float32 [1024, 1024], P(('dp', 'seq'))
- self_text_proj_grad: float32 [3, 768, 768], P(None, None, ('dp', 'seq'))
- self_text_out_grad: float32 [768, 768], P(('dp', 'seq'))
- self_text_up_grad: float32 [768, 3072], P(None, ('dp', 'seq'))
- self_text_down_grad: float32 [3072, 768], P(None, ('dp', 'seq'))
- self_image_proj_grad: float32 [3, 1024, 1024], P(None, None, ('dp', 'seq'))
- self_image_out_grad: float32 [1024, 1024], P(('dp', 'seq'))
- self_image_up_grad: float32 [1024, 1024], P(None, ('dp', 'seq'))
- self_image_down_grad: float32 [1024, 1024], P(None, ('dp', 'seq'))
- text_gains_grad: float32 [4, 768], P(None, ('dp', 'seq'))
- image_gains_grad: float32 [4, 1024], P(None, ('dp', 'seq'))
The draws below stay inside these ranges and needn't reach their ends.
Inputs may be any that keep to these rules, and one draw needn't show every extreme that they name: A pair's caption uses its first caption_lengths tokens; some pair in every draw uses all 100.
All inputs are finite; a program needn't handle non-finite values.
Results may differ from the reference program's by a relative error of at most 0.024.
Values may be sent and summed in bfloat16 or wider, within the bound.
No kernel may reach another device: no remote copies, remote signals or barrier semaphores. Data moves between devices by JAX's collectives and lax.ppermute only.
A program may use at most 320 MiB of HBM per device.

```python
import jax
import jax.numpy as jnp
from jax import lax

D_T = 768
D_V = 1024
CO_WIDTH = 1024
FF_T = 3072
FF_V = 1024
H_T = 12
H_V = 8
H_C = 8
L_T = 100
L_V = 36
P_DEV = 2
PAIRS = 32


def draw_caption_lengths(key, part):
    key = jax.random.fold_in(key, 7)
    first_key, second_key = jax.random.split(key)
    drawn = jax.random.randint(first_key, (PAIRS,), 1, L_T + 1)
    chosen = jax.random.randint(second_key, (), 0, PAIRS)
    return jnp.where(jnp.arange(PAIRS) == chosen, L_T, drawn).astype(jnp.int32)


def strengthened(values, key, source, target, shards_of, factor):
    def block_of(dim):
        return (jnp.arange(values.shape[dim]) // (values.shape[dim] // shards_of)).reshape((-1,) + (1,) * (values.ndim - 1 - dim))

    first = jax.random.permutation(key, shards_of)[block_of(target)]
    other_side = (block_of(target) + shards_of // 2) % shards_of
    return jnp.where((block_of(source) == first) | (block_of(source) == other_side), factor * values, values)


def level_of(key, extent, pieces, low, high):
    def one(dim, shards_of):
        heights = jax.random.uniform(jax.random.fold_in(jax.random.fold_in(key, 6), dim), (shards_of,), jnp.float32, low / len(pieces), high / len(pieces))
        return jnp.repeat(jnp.exp(heights), extent[dim] // shards_of).reshape((-1,) + (1,) * (len(extent) - dim - 1))

    gain = one(*pieces[0])
    for cut in pieces[1:]:
        gain = gain * one(*cut)
    return gain


def gaussian(stream_key, shape, scale, bound, cuts=(), kind=jnp.bfloat16):
    values = scale * jax.random.normal(stream_key, shape, jnp.float32)
    if cuts:
        values = values * level_of(stream_key, shape, cuts, -0.22, 0.18)
    return jnp.clip(values, -bound, bound).astype(kind)


def noise_with(own_key, shape, deviation, limit, cuts, heavy, kind=jnp.bfloat16):
    values = deviation * jax.random.normal(own_key, shape, jnp.float32)
    if cuts:
        values = values * level_of(own_key, shape, cuts, -0.22, 0.18)
    return jnp.clip(strengthened(values, jax.random.fold_in(own_key, 3), *heavy), -limit, limit).astype(kind)


def setup_inputs(seed: int = 0) -> dict:
    key_of = jax.random.split(jax.random.key(seed), 24)
    text_input = gaussian(key_of[0], (PAIRS, L_T, D_T), 1.0, 6.0, ((0, 32),))
    image_input = gaussian(key_of[1], (PAIRS, L_V, D_V), 1.0, 6.0, ((0, 32),))
    caption_lengths = draw_caption_lengths(jax.random.fold_in(key_of[23], 71), 0)
    text_cotangent = noise_with(key_of[3], (PAIRS, L_T, D_T), 1.0, 6.0, ((0, 32),), (0, 2, 32, 2.75))
    image_cotangent = noise_with(key_of[4], (PAIRS, L_V, D_V), 1.0, 6.0, ((0, 32),), (0, 2, 32, 2.75))
    cross_text_proj = gaussian(key_of[5], (3, D_T, CO_WIDTH), D_T ** -0.5, 0.21875, ((1, 32),))
    cross_image_proj = gaussian(key_of[6], (3, D_V, CO_WIDTH), D_V ** -0.5, 0.1875, ((1, 32),))
    cross_text_out = gaussian(key_of[7], (CO_WIDTH, D_T), (CO_WIDTH // 6) ** -0.5, 0.4375, ((0, 32),))
    cross_image_out = gaussian(key_of[8], (CO_WIDTH, D_V), (CO_WIDTH // 7) ** -0.5, 0.5, ((0, 32),))
    cross_text_up = gaussian(key_of[9], (D_T, FF_T), D_T ** -0.5, 0.21875, ((0, 32),))
    cross_text_down = gaussian(key_of[10], (FF_T, D_T), FF_T ** -0.5, 0.109375, ((0, 32),))
    cross_image_up = gaussian(key_of[11], (D_V, FF_V), D_V ** -0.5, 0.1875, ((0, 32),))
    cross_image_down = gaussian(key_of[12], (FF_V, D_V), FF_V ** -0.5, 0.1875, ((0, 32),))
    self_text_proj = gaussian(key_of[13], (3, D_T, D_T), D_T ** -0.5, 0.21875, ((1, 32),))
    self_text_out = gaussian(key_of[14], (D_T, D_T), (D_T // 7) ** -0.5, 0.5, ((0, 32),))
    self_text_up = gaussian(key_of[15], (D_T, FF_T), D_T ** -0.5, 0.21875, ((0, 32),))
    self_text_down = gaussian(key_of[16], (FF_T, D_T), FF_T ** -0.5, 0.109375, ((0, 32),))
    self_image_proj = gaussian(key_of[17], (3, D_V, D_V), D_V ** -0.5, 0.1875, ((1, 32),))
    self_image_out = gaussian(key_of[18], (D_V, D_V), (D_V // 6) ** -0.5, 0.4375, ((0, 32),))
    self_image_up = gaussian(key_of[19], (D_V, FF_V), D_V ** -0.5, 0.1875, ((0, 32),))
    self_image_down = gaussian(key_of[20], (FF_V, D_V), FF_V ** -0.5, 0.1875, ((0, 32),))
    text_gains = jnp.clip(1.0 + 0.1 * jax.random.normal(key_of[21], (4, D_T), jnp.float32), 0.5, 1.5)
    image_gains = jnp.clip(1.0 + 0.1 * jax.random.normal(key_of[22], (4, D_V), jnp.float32), 0.5, 1.5)
    return dict(text_input=text_input, image_input=image_input, caption_lengths=caption_lengths, text_cotangent=text_cotangent, image_cotangent=image_cotangent, cross_text_proj=cross_text_proj, cross_image_proj=cross_image_proj, cross_text_out=cross_text_out, cross_image_out=cross_image_out, cross_text_up=cross_text_up, cross_text_down=cross_text_down, cross_image_up=cross_image_up, cross_image_down=cross_image_down, self_text_proj=self_text_proj, self_text_out=self_text_out, self_text_up=self_text_up, self_text_down=self_text_down, self_image_proj=self_image_proj, self_image_out=self_image_out, self_image_up=self_image_up, self_image_down=self_image_down, text_gains=text_gains, image_gains=image_gains)


EPSILON = 1e-05
NEGATIVE = -1000000000.0

@jax.custom_vjp
def low(v):
    return lax.optimization_barrier(v.astype(jnp.bfloat16)).astype(jnp.float32)

@jax.custom_vjp
def low_back(v):
    return v

def low_keep(v):
    return (low(v), None)

def low_pass(kept, grad):
    return (grad,)

def back_keep(v):
    return (v, None)

def back_low(kept, grad):
    return (low(grad),)
low.defvjp(low_keep, low_pass)
low_back.defvjp(back_keep, back_low)

def matmul(left, right):
    return jnp.einsum('...k,kn->...n', left, right, precision=lax.Precision.HIGHEST)

def layer_norm(stream, gain_vec):
    center = stream - lax.optimization_barrier(jnp.mean(stream, axis=-1, keepdims=True))
    spread = lax.optimization_barrier(jnp.mean(center * center, axis=-1, keepdims=True))
    return center * lax.rsqrt(spread + EPSILON) * gain_vec

def heads_of(stream, heads):
    return stream.reshape(stream.shape[0], stream.shape[1], heads, stream.shape[2] // heads)

def attend(queries, key_rows, value_rows, valid_keys, heads):
    size_head = queries.shape[-1] // heads
    query_heads = heads_of(queries, heads)
    key_heads = heads_of(key_rows, heads)
    value_heads = heads_of(value_rows, heads)
    scores = jnp.einsum('pqhd,pkhd->phqk', query_heads, key_heads, precision=lax.Precision.HIGHEST) * size_head ** (-0.5)
    scores = low_back(scores)
    scores = jnp.where(valid_keys[:, None, None, :], scores, NEGATIVE)
    maxima = lax.optimization_barrier(jnp.max(scores, axis=-1, keepdims=True))
    expo_terms = jnp.exp(scores - maxima)
    attn_probs = low(expo_terms / lax.optimization_barrier(jnp.sum(expo_terms, axis=-1, keepdims=True)))
    mixed = jnp.einsum('phqk,pkhd->pqhd', attn_probs, value_heads, precision=lax.Precision.HIGHEST)
    return mixed.reshape(queries.shape[0], queries.shape[1], queries.shape[2])

def project(stream, weights):
    stream_low = low(stream)
    return [low(low_back(matmul(stream_low, weights[member]))) for member in range(3)]

def tail(residual, mixed, out_mat, up_mat, down_mat, gain_pair):
    attn_low = low(low_back(mixed))
    first_norm = layer_norm(residual + low_back(matmul(attn_low, out_mat)), gain_pair[0])
    upper = low_back(matmul(low(first_norm), up_mat))
    active = low(jax.nn.gelu(upper))
    return layer_norm(first_norm + low_back(matmul(active, down_mat)), gain_pair[1])

def self_block(stream, proj_mat, out_mat, up_mat, down_mat, gain_pair, heads, valid_keys):
    queries, key_rows, value_rows = project(stream, proj_mat)
    mixed = attend(queries, key_rows, value_rows, valid_keys, heads)
    return tail(stream, mixed, out_mat, up_mat, down_mat, gain_pair)

def forward(weights, text_stream, image_stream, length_part):
    cross_text_proj, cross_image_proj, cross_text_out, cross_image_out, cross_text_up, cross_text_down, cross_image_up, cross_image_down, self_text_proj, self_text_out, self_text_up, self_text_down, self_image_proj, self_image_out, self_image_up, self_image_down, text_gains, image_gains = weights
    text_valid = jnp.arange(text_stream.shape[1])[None, :] < length_part[:, None]
    image_valid = jnp.ones((image_stream.shape[0], image_stream.shape[1]), dtype=jnp.bool_)
    text_query, text_key, text_value = project(text_stream, cross_text_proj)
    image_query, image_key, image_value = project(image_stream, cross_image_proj)
    text_mixed = attend(text_query, image_key, image_value, image_valid, H_C)
    image_mixed = attend(image_query, text_key, text_value, text_valid, H_C)
    text_cross = tail(text_stream, text_mixed, cross_text_out, cross_text_up, cross_text_down, text_gains[0:2])
    image_cross = tail(image_stream, image_mixed, cross_image_out, cross_image_up, cross_image_down, image_gains[0:2])
    text_final = self_block(text_cross, self_text_proj, self_text_out, self_text_up, self_text_down, text_gains[2:4], H_T, text_valid)
    image_final = self_block(image_cross, self_image_proj, self_image_out, self_image_up, self_image_down, image_gains[2:4], H_V, image_valid)
    return (text_final, image_final)

def reference(text_input, image_input, caption_lengths, text_cotangent, image_cotangent, cross_text_proj, cross_image_proj, cross_text_out, cross_image_out, cross_text_up, cross_text_down, cross_image_up, cross_image_down, self_text_proj, self_text_out, self_text_up, self_text_down, self_image_proj, self_image_out, self_image_up, self_image_down, text_gains, image_gains):
    weights = tuple((member.astype(jnp.float32) for member in (cross_text_proj, cross_image_proj, cross_text_out, cross_image_out, cross_text_up, cross_text_down, cross_image_up, cross_image_down, self_text_proj, self_text_out, self_text_up, self_text_down, self_image_proj, self_image_out, self_image_up, self_image_down, text_gains, image_gains)))
    groups = text_input.shape[0] // P_DEV

    def regroup(array):
        return array.reshape((groups, P_DEV) + array.shape[1:])

    def scan_step(carried, batch_part):
        text_part, image_part, length_part, text_grad, image_grad = batch_part

        def run_layer(weight_set, text_stream, image_stream):
            return forward(weight_set, text_stream, image_stream, length_part)
        outputs, pullback = jax.vjp(run_layer, weights, text_part.astype(jnp.float32), image_part.astype(jnp.float32))
        weight_grads, text_back, image_back = pullback((text_grad.astype(jnp.float32), image_grad.astype(jnp.float32)))
        carried = jax.tree.map(jnp.add, carried, weight_grads)
        return (carried, (outputs[0].astype(jnp.bfloat16), outputs[1].astype(jnp.bfloat16), text_back, image_back))
    zero_grads = tuple((jnp.zeros_like(member) for member in weights))
    summed, (text_out, image_out, text_back, image_back) = lax.scan(scan_step, zero_grads, (regroup(text_input), regroup(image_input), regroup(caption_lengths), regroup(text_cotangent), regroup(image_cotangent)))
    return (text_out.reshape(text_input.shape), image_out.reshape(image_input.shape), text_back.reshape(text_input.shape), image_back.reshape(image_input.shape), summed[0], summed[1], summed[2], summed[3], summed[4], summed[5], summed[6], summed[7], summed[8], summed[9], summed[10], summed[11], summed[12], summed[13], summed[14], summed[15], summed[16], summed[17])
```

```python
import jax
import jax.numpy as jnp
from jax import lax
from jax.experimental import pallas as pl
from jax.experimental.pallas import tpu as pltpu
from jax.sharding import PartitionSpec as P

H_T = 12
H_V = 8
H_C = 8

EPSILON = 1e-05
NEGATIVE = -1000000000.0
FLOAT = jnp.float32
BFLOAT = jnp.bfloat16
ALL = ("dp", "seq")
FREE = pl.CostEstimate(flops=0, bytes_accessed=0, transcendentals=0)


def device_bits():
    return (lax.axis_size("dp").bit_length() - 1, lax.axis_size("seq").bit_length() - 1)


def my_index():
    return lax.axis_index("dp") * lax.axis_size("seq") + lax.axis_index("seq")


def swap(block, bit):
    size = lax.axis_size("dp") * lax.axis_size("seq")
    return lax.ppermute(block, ALL, [(i, i ^ (1 << bit)) for i in range(size)])


def orders():
    dp_bits, seq_bits = device_bits()
    total = dp_bits + seq_bits
    core = seq_bits
    rest = [b for b in range(total) if b != core]
    seq_first = [core] + rest
    dp_first = [core] + rest[1:2] + rest[0:1] + rest[2:]
    far_first = [core] + rest[2:3] + rest[1:2] + rest[0:1] + rest[3:]
    return seq_first, dp_first, far_first


def take(block, which):
    return lax.dynamic_index_in_dim(block, which, 0, keepdims=False)


def add_low(left, right):
    return (left.astype(FLOAT) + right.astype(FLOAT)).astype(BFLOAT)


def join_blocks(held, came, order, splits):
    count, rows, width = held.shape
    bits = len(order)
    near = order.index(0)
    low = 1 << near
    pairs = (count // (2 * low), 2, low, rows, width)

    def out_index(j, at):
        place = jnp.int32(0)
        for k, b in enumerate(order[:-1]):
            if b != 0:
                bit = lax.rem(lax.shift_right_logical(j, k if k < near else k - 1), 2)
                place = place + lax.shift_left(bit, b)
        block = jnp.bitwise_xor(at[0], place)
        return (lax.shift_right_logical(block, 2), 0, 0, 0, 0)

    def body(at_ref, held_ref, came_ref, *outs):
        side = lax.rem(lax.shift_right_logical(at_ref[0], 1), 2)
        mine = lax.rem(at_ref[0], 2)
        start = 0
        for out, many in zip(outs, splits):
            for step in range(2):
                y = jnp.bitwise_xor(mine, step)
                out[0, side, y] = held_ref[0, step, 0, start : start + many]
                out[0, 1 - side, y] = came_ref[0, step, 0, start : start + many]
            start += many

    def in_index(j, at):
        return (lax.div(j, low), 0, lax.rem(j, low), 0, 0)

    outs = pl.pallas_call(
        body,
        grid_spec=pltpu.PrefetchScalarGridSpec(
            num_scalar_prefetch=1,
            grid=(count // 2,),
            in_specs=[pl.BlockSpec((1, 2, 1, rows, width), in_index)] * 2,
            out_specs=[pl.BlockSpec((1, 2, 2, many, width), out_index) for many in splits],
        ),
        out_shape=[
            jax.ShapeDtypeStruct((1 << (bits - 2), 2, 2, many, width), held.dtype) for many in splits
        ],
        compiler_params=pltpu.CompilerParams(vmem_limit_bytes=32 * 1024 * 1024),
        cost_estimate=FREE,
    )(my_index().astype(jnp.int32).reshape(1), held.reshape(pairs), came.reshape(pairs))
    return [out.reshape(-1, width) for out in outs]


class Gather:
    def __init__(self, shard, order, splits=None):
        self.order = order
        self.held = shard[None]
        self.splits = splits or [shard.shape[0]]
        self.step = 0

    def start(self):
        self.came = swap(self.held, self.order[self.step])
        self.step += 1

    def absorb(self):
        if self.step == len(self.order):
            self.full = join_blocks(self.held, self.came, self.order, self.splits)
        else:
            self.held = jnp.concatenate([self.held, self.came], axis=0)


def close_round(movers, *arrays):
    came = [m.came for m in movers]
    came, arrays = lax.optimization_barrier((came, arrays))
    for m, block in zip(movers, came):
        m.came = block
    for m in movers:
        m.absorb()
    return arrays


def sides_of(order):
    at = my_index()
    return [lax.rem(lax.shift_right_logical(at, b), 2) for b in order]


def panels_of(other, width):
    return other.shape[1] // width


def rows_in_order(rows, first, own, size, order):
    total = len(order)
    part = rows[:, first : first + own * size]
    split = part.reshape((part.shape[0],) + (2,) * total + (own,))
    axes = [1 + (total - 1 - b) for b in order] + [1 + total, 0]
    return split.transpose(axes).reshape(size * own, part.shape[0])


def pack_plain(items, width, order):
    size = 1 << len(order)
    parts = []
    for rows, first, span, other in items:
        own = span // size
        block = mm(rows_in_order(rows, first, own, size, order), other).astype(BFLOAT)
        block = block.reshape(size, own, panels_of(other, width), width).transpose(0, 2, 1, 3)
        parts.append(block.reshape(size, -1, width))
    return jnp.concatenate(parts, axis=1)


def pack_kernel(items, width, order, natural):
    total = len(order)
    size = 1 << total
    groups = size // 4
    core_side = sides_of(order[:1])[0]
    owns = [span // size for rows, first, span, other in items]
    panels = [panels_of(other, width) for rows, first, span, other in items]
    count = len(items)
    total_rows = sum(o * p for o, p in zip(owns, panels))
    lefts, left_specs = [], []
    for (rows, first, span, other), own in zip(items, owns):
        length = rows.shape[0]
        at = first // (4 * own)
        if (4 * own) % 128 == 0:
            lefts.append(rows)
            left_specs.append(pl.BlockSpec((length, 4 * own), lambda g, core, at=at: (0, at + g)))
        else:
            lefts.append(rows.reshape(length, -1, 4 * own).transpose(1, 0, 2))
            left_specs.append(pl.BlockSpec((None, length, 4 * own), lambda g, core, at=at: (at + g, 0, 0)))
    rights, used = [], []
    for item in items:
        match = [i for i, other in enumerate(rights) if other is item[3]]
        if not match:
            rights.append(item[3])
        used.append(match[0] if match else len(rights) - 1)
    right_specs = [pl.BlockSpec(other.shape, lambda g, core: (0, 0)) for other in rights]
    rest = order[1:]

    def out_index(g, core):
        return tuple(0 if b == 0 else lax.rem(lax.shift_right_logical(g, b - 2), 2) for b in rest) + (0, 0)

    out_shape = (2,) * len(rest) + (total_rows, width)
    out_block = tuple(2 if b == 0 else None for b in rest) + (total_rows, width)
    outs = 1 if natural else 2
    if natural:
        out_shape = (size, total_rows, width)
        out_block = (4, total_rows, width)
        out_index = lambda g, core: (g, 0, 0)

    def body(core_ref, *refs):
        left_refs = refs[:count]
        right_refs = refs[count : count + len(rights)]
        pack_refs = refs[count + len(rights) : count + len(rights) + outs]
        held = refs[count + len(rights) + outs :]
        core = core_ref[0]
        for left, right, keepers in zip(left_refs, used, held):
            keepers[...] = t_mm(left[...], right_refs[right][...])
        if natural:
            targets = [(pack_refs[0], i, i) for i in range(4)]
        else:
            targets = [(pack_refs[0], i, 2 * (1 - core) + i) for i in range(2)]
            targets += [(pack_refs[1], i, 2 * core + i) for i in range(2)]
        for ref, near, which in targets:
            pieces = []
            for keepers, own, many in zip(held, owns, panels):
                start = which * own if natural else pl.multiple_of(which * own, 8)
                for p in range(many):
                    pieces.append(keepers[pl.ds(start, own), p * width : (p + 1) * width])
            ref[near] = jnp.concatenate(pieces, axis=0).astype(BFLOAT)

    flops = sum(2 * rows.shape[0] * span * other.shape[1] for rows, first, span, other in items)
    packed = pl.pallas_call(
        body,
        grid_spec=pltpu.PrefetchScalarGridSpec(
            num_scalar_prefetch=1,
            grid=(groups,),
            in_specs=left_specs + right_specs,
            out_specs=[pl.BlockSpec(out_block, out_index)] * outs,
            scratch_shapes=[
                pltpu.VMEM((4 * own, other.shape[1]), FLOAT)
                for own, (rows, first, span, other) in zip(owns, items)
            ],
        ),
        out_shape=[jax.ShapeDtypeStruct(out_shape, BFLOAT)] * outs,
        compiler_params=pltpu.CompilerParams(vmem_limit_bytes=32 * 1024 * 1024),
        cost_estimate=FREE,
    )(core_side.astype(jnp.int32).reshape(1), *lefts, *rights)
    if natural:
        return packed[0]
    flat = (size // 2, total_rows, width)
    return packed[0].reshape(flat), packed[1].reshape(flat)


def aligned_items(items, size):
    return all(span % (8 * size) == 0 for rows, first, span, other in items)


def pack_natural(items, width):
    bits = sum(device_bits())
    if aligned_items(items, 1 << bits):
        return pack_kernel(items, width, list(range(bits)), True)
    return pack_plain(items, width, list(range(bits))[::-1])


def pack(items, width, order):
    size = 1 << len(order)
    if aligned_items(items, size) and order[0] == 1:
        return pack_kernel(items, width, order, False)
    block = pack_plain(items, width, order)
    block = block.reshape((2, size // 2) + block.shape[1:])
    at = sides_of(order[:1])[0]
    return take(block, 1 - at), take(block, at)


class Whole:
    def __init__(self, items, width):
        self.block = pack_natural(items, width)

    def launch(self):
        flat = self.block.reshape(-1, self.block.shape[-1])
        self.sum = lax.psum_scatter(flat, ALL, scatter_dimension=0, tiled=True)

    def finish(self):
        return self.sum.astype(FLOAT)


class Chunk:
    def __init__(self, items, width, order):
        self.order = order
        self.sides = sides_of(order)
        self.send, self.keep = pack(items, width, order)
        self.step = 0

    def start(self):
        self.came = swap(self.send, self.order[self.step])
        self.step += 1

    def absorb(self):
        if self.step == len(self.order):
            self.full = (self.came.astype(FLOAT) + self.keep.astype(FLOAT))[0]
            return
        half = self.came.shape[0] // 2
        came = self.came.reshape((2, half) + self.came.shape[1:])
        keep = self.keep.reshape((2, half) + self.keep.shape[1:])
        at = self.sides[self.step]
        self.send = add_low(take(came, 1 - at), take(keep, 1 - at))
        self.keep = add_low(take(came, at), take(keep, at))


class Small(Chunk):
    def __init__(self, block, order):
        total = len(order)
        tail = block.shape[1:]
        held = block.reshape((2,) * total + tail)
        held = held.transpose([total - 1 - b for b in order] + [total + i for i in range(len(tail))])
        held = held.reshape((2, -1) + tail)
        self.order = order
        self.sides = sides_of(order)
        self.send, self.keep = take(held, 1 - self.sides[0]), take(held, self.sides[0])
        self.step = 0


def mm(left, right):
    return jnp.dot(left, right, preferred_element_type=FLOAT)


def mm_t(left, right):
    return lax.dot_general(left, right, (((1,), (1,)), ((), ())), preferred_element_type=FLOAT)


def t_mm(left, right):
    return lax.dot_general(left, right, (((0,), (0,)), ((), ())), preferred_element_type=FLOAT)


def layer_norm(stream, gain_vec):
    center = stream - jnp.mean(stream, axis=-1, keepdims=True)
    spread = jnp.mean(center * center, axis=-1, keepdims=True)
    return center * lax.rsqrt(spread + EPSILON) * gain_vec


def norm_back(stream, gain_vec, upstream):
    center = stream - jnp.mean(stream, axis=-1, keepdims=True)
    scale = lax.rsqrt(jnp.mean(center * center, axis=-1, keepdims=True) + EPSILON)
    unit = center * scale
    weighted = upstream * gain_vec
    inner = jnp.mean(weighted * unit, axis=-1, keepdims=True)
    grad = (weighted - jnp.mean(weighted, axis=-1, keepdims=True) - unit * inner) * scale
    return grad, (upstream * unit).astype(BFLOAT)


def gelu_back(upper, upstream):
    unused, pullback = jax.vjp(jax.nn.gelu, upper)
    return pullback(upstream)[0]


def head_blocks(width, heads):
    size = width // heads
    block = max(size, 128)
    return [(h * size // block * block, block, h * size % block, size) for h in range(heads)]


def only_head(value, start, size):
    if size == value.shape[1]:
        return value
    lane = lax.broadcasted_iota(jnp.int32, value.shape, 1)
    return jnp.where((lane >= start) & (lane < start + size), value, jnp.zeros_like(value))


def head_probs(query, key, size, valid):
    scores = mm_t(query, key) * (size ** (-0.5))
    if valid is not None:
        lane = lax.broadcasted_iota(jnp.int32, scores.shape, 1)
        scores = jnp.where(lane < valid, scores, NEGATIVE)
    expo = jnp.exp(scores - jnp.max(scores, axis=-1, keepdims=True))
    return expo / jnp.sum(expo, axis=-1, keepdims=True)


def attend_block(q_ref, k_ref, v_ref, q_at, k_at, v_at, out_ref, heads, valid):
    width = out_ref.shape[1]
    parts = {}
    for base, block, start, size in head_blocks(width, heads):
        q = only_head(q_ref[:, q_at + base : q_at + base + block], start, size)
        k = k_ref[:, k_at + base : k_at + base + block]
        v = only_head(v_ref[:, v_at + base : v_at + base + block], start, size)
        part = mm(head_probs(q, k, size, valid).astype(BFLOAT), v)
        parts[base] = part if base not in parts else parts[base] + part
        if start + size == block:
            out_ref[:, base : base + block] = parts[base].astype(BFLOAT)


def attend_block_back(
    q_ref, k_ref, v_ref, q_at, k_at, v_at, g_ref, dq_ref, dk_ref, dv_ref, heads, valid
):
    width = g_ref.shape[1]
    parts = {}
    for base, block, start, size in head_blocks(width, heads):
        q = only_head(q_ref[:, q_at + base : q_at + base + block], start, size)
        k = only_head(k_ref[:, k_at + base : k_at + base + block], start, size)
        v = v_ref[:, v_at + base : v_at + base + block]
        g = only_head(g_ref[:, base : base + block], start, size)
        probs = head_probs(q, k, size, valid)
        grad_probs = mm_t(g, v)
        inner = jnp.sum(grad_probs * probs, axis=-1, keepdims=True)
        grad_scores = (probs * (grad_probs - inner)).astype(BFLOAT)
        scale = size ** (-0.5)
        news = (mm(grad_scores, k) * scale, t_mm(grad_scores, q) * scale, t_mm(probs.astype(BFLOAT), g))
        if base in parts:
            news = tuple(x + y for x, y in zip(parts[base], news))
        parts[base] = news
        if start + size == block:
            for ref, at, new in zip((dq_ref, dk_ref, dv_ref), (q_at, k_at, v_at), news):
                ref[:, at + base : at + base + block] = new.astype(BFLOAT)


def vmem_call(body, count, outs, scalar, flops, *operands):
    return pl.pallas_call(
        body,
        in_specs=[pl.BlockSpec(memory_space=pltpu.SMEM)] + [pl.BlockSpec(memory_space=pltpu.VMEM)] * count,
        out_specs=[pl.BlockSpec(memory_space=pltpu.VMEM)] * len(outs),
        out_shape=[jax.ShapeDtypeStruct(shape, BFLOAT) for shape in outs],
        compiler_params=pltpu.CompilerParams(vmem_limit_bytes=32 * 1024 * 1024),
        cost_estimate=FREE,
    )(scalar, *operands)


def cross_attend(text, image, length):
    width = text.shape[1] // 3

    def body(len_ref, text_ref, image_ref, t_ref, i_ref):
        attend_block(text_ref, image_ref, image_ref, 0, width, 2 * width, t_ref, H_C, None)
        attend_block(image_ref, text_ref, text_ref, 0, width, 2 * width, i_ref, H_C, len_ref[0])

    flops = 8 * text.shape[0] * image.shape[0] * width * 8
    outs = [(text.shape[0], width), (image.shape[0], width)]
    return vmem_call(body, 2, outs, length, flops, text, image)


def cross_attend_back(text, image, length, t_grad, i_grad):
    width = text.shape[1] // 3

    def body(len_ref, text_ref, image_ref, tg_ref, ig_ref, dt_ref, di_ref):
        attend_block_back(
            text_ref, image_ref, image_ref, 0, width, 2 * width, tg_ref, dt_ref, di_ref, di_ref, H_C, None
        )
        attend_block_back(
            image_ref, text_ref, text_ref, 0, width, 2 * width, ig_ref, di_ref, dt_ref, dt_ref, H_C, len_ref[0]
        )

    flops = 20 * text.shape[0] * image.shape[0] * width * 8
    return vmem_call(body, 4, [text.shape, image.shape], length, flops, text, image, t_grad, i_grad)


def self_attend(packed, heads, length, masked):
    width = packed.shape[1] // 3

    def body(len_ref, ref, out_ref):
        attend_block(ref, ref, ref, 0, width, 2 * width, out_ref, heads, len_ref[0] if masked else None)

    flops = 4 * packed.shape[0] * packed.shape[0] * width * 8
    return vmem_call(body, 1, [(packed.shape[0], width)], length, flops, packed)[0]


def self_attend_back(packed, heads, length, masked, grad):
    width = packed.shape[1] // 3

    def body(len_ref, ref, g_ref, d_ref):
        attend_block_back(
            ref, ref, ref, 0, width, 2 * width, g_ref, d_ref, d_ref, d_ref, heads, len_ref[0] if masked else None
        )

    flops = 10 * packed.shape[0] * packed.shape[0] * width * 8
    return vmem_call(body, 2, [packed.shape], length, flops, packed, grad)[0]


def tail_forward(residual, attn_low, out_mat, up_mat, down_mat, gain_pair):
    first_sum = residual + mm(attn_low, out_mat)
    first_norm = layer_norm(first_sum, gain_pair[0])
    hidden_low = first_norm.astype(BFLOAT)
    upper = mm(hidden_low, up_mat)
    active = jax.nn.gelu(upper).astype(BFLOAT)
    second_sum = first_norm + mm(active, down_mat)
    return layer_norm(second_sum, gain_pair[1]), (first_sum, hidden_low, upper, active, second_sum)


def tail_backward(grad_result, kept, attn_low, out_mat, up_mat, down_mat, gain_pair, down_natural):
    first_sum, hidden_low, upper, active, second_sum = kept
    grad_second, gain_two = norm_back(second_sum, gain_pair[1], grad_result)
    low = grad_second.astype(BFLOAT)
    grad_down = whole_item(active, low) if down_natural else whole_item(low, active)
    grad_upper = gelu_back(upper, mm_t(low, down_mat)).astype(BFLOAT)
    grad_up = whole_item(grad_upper, hidden_low)
    grad_norm = grad_second + mm_t(grad_upper, up_mat)
    grad_first, gain_one = norm_back(first_sum, gain_pair[0], grad_norm)
    grad_first_low = grad_first.astype(BFLOAT)
    grad_out = whole_item(attn_low, grad_first_low)
    grad_attn = mm_t(grad_first_low, out_mat).astype(BFLOAT)
    return grad_first, grad_attn, [grad_down, grad_up, grad_out], [gain_one, gain_two]


def project(stream_low, proj):
    return mm(stream_low, proj).astype(BFLOAT)


def whole_item(rows, other):
    return (rows, 0, rows.shape[1], other)


def third_items(packed, other):
    span = packed.shape[1] // 3
    return [(packed, e * span, span, other) for e in range(3)]


def side(shards):
    return jnp.concatenate(shards, axis=1)


def on_device(
    text_input,
    image_input,
    caption_lengths,
    text_cotangent,
    image_cotangent,
    cross_text_proj,
    cross_image_proj,
    cross_text_out,
    cross_image_out,
    cross_text_up,
    cross_text_down,
    cross_image_up,
    cross_image_down,
    self_text_proj,
    self_text_out,
    self_text_up,
    self_text_down,
    self_image_proj,
    self_image_out,
    self_image_up,
    self_image_down,
    text_gains,
    image_gains,
):
    d_t = text_input.shape[2]
    d_v = image_input.shape[2]
    co = cross_text_proj.shape[2]
    ff_t = cross_text_up.shape[1]
    n_text = text_input.shape[1]

    size = lax.axis_size("dp") * lax.axis_size("seq")
    bits = sum(device_bits())
    by_permute = size == 1 << bits and all(
        m.shape[-2] % 8 == 0 for m in (cross_text_out, cross_text_down, self_text_down)
    )

    def gather_columns(parts):
        return lax.all_gather(side(parts), ALL, axis=0, tiled=True)

    own_t, own_v = d_t // size, d_v // size
    own_f, own_c = ff_t // size, co // size
    text_parts = list(cross_text_proj) + [cross_text_up] + list(self_text_proj)
    text_wide = gather_columns(text_parts + [self_text_out, self_text_up])
    image_parts = [cross_image_out, cross_image_up, cross_image_down] + list(self_image_proj)
    image_wide = gather_columns(image_parts + [self_image_out, self_image_up, self_image_down])
    w_ctp = text_wide[:, : 3 * co]

    high = list(range(3, bits))[::-1]
    x_first = high + [2, 0, 1]
    y_first = high + [0, 2, 1]
    shards = [
        (side(list(cross_image_proj)), y_first, None),
        (jnp.concatenate([cross_text_down, cross_text_out], axis=0), x_first, [own_f, own_c]),
        (self_text_down, x_first, None),
    ]

    panel = 128
    my_len = lax.dynamic_index_in_dim(caption_lengths, lax.axis_index("seq"), 0, keepdims=True)
    x_t = text_input[0]
    x_v = image_input[0]

    if by_permute:
        movers = [Gather(*item) for item in shards]
        for turn_at in range(bits):
            active = movers[:2] + ([movers[2]] if turn_at >= 2 else [])
            for m in active:
                m.start()
            close_round(active)
        w_cip = movers[0].full[0]
        w_ctd, w_cto = movers[1].full
        movers[2].start()
        t_packed = project(x_t, w_ctp)
        i_packed = project(x_v, w_cip)
        t_attn, i_attn = cross_attend(t_packed, i_packed, my_len)
        t_attn, i_attn = close_round(movers[2:], t_attn, i_attn)
        movers[2].start()
    else:
        full = [lax.all_gather(shard, ALL, axis=0) for shard, order, splits in shards]
        w_ctd, w_cto = full[1][:, :own_f], full[1][:, own_f:]
        w_cip, w_ctd, w_cto, w_std = (w.reshape(-1, w.shape[-1]) for w in (full[0], w_ctd, w_cto, full[2]))
        t_packed = project(x_t, w_ctp)
        i_packed = project(x_v, w_cip)
        t_attn, i_attn = cross_attend(t_packed, i_packed, my_len)

    w_ctu = text_wide[:, 3 * co : 3 * co + ff_t]
    text_self = text_wide[:, 3 * co + ff_t :]
    w_stp, w_sto, w_stu = text_self[:, : 3 * d_t], text_self[:, 3 * d_t : 4 * d_t], text_self[:, 4 * d_t :]

    def halving(*picks):
        return [1] + list(picks) + [b for b in range(bits) if b != 1 and b not in picks]

    t_cross, t_kept = tail_forward(x_t.astype(FLOAT), t_attn, w_cto, w_ctu, w_ctd, text_gains[0:2])
    t_low = t_cross.astype(BFLOAT)
    if by_permute:
        t_cross, t_kept = close_round(movers[2:], t_cross, t_kept)
        w_std = movers[2].full[0]
        t_low = t_cross.astype(BFLOAT)
    st_packed = project(t_low, w_stp)
    st_attn = self_attend(st_packed, H_T, my_len, True)
    t_final, st_kept = tail_forward(t_cross, st_attn, w_sto, w_stu, w_std, text_gains[2:4])
    t_res, t_ga, t_pairs, t_gain_s = tail_backward(
        text_cotangent[0].astype(FLOAT), st_kept, st_attn, w_sto, w_stu, w_std, text_gains[2:4], False
    )
    c1t = Whole(t_pairs, d_t)
    c1t.block, t_ga, t_res, i_attn = close_round([], c1t.block, t_ga, t_res, i_attn)
    c1t.launch()
    st_grads = self_attend_back(st_packed, H_T, my_len, True, t_ga)
    t_back = t_res + mm_t(st_grads, w_stp)
    c2t = Chunk(third_items(st_grads, t_low), d_t, halving(2, 3, 0))
    c2t.send, c2t.keep, t_back, i_attn = close_round([], c2t.send, c2t.keep, t_back, i_attn)

    w_cio, w_ciu, w_cid = (image_wide[:, i * d_v : (i + 1) * d_v] for i in range(3))
    w_sip = image_wide[:, 3 * d_v : 6 * d_v]
    w_sio, w_siu, w_sid = (image_wide[:, (6 + i) * d_v : (7 + i) * d_v] for i in range(3))

    c2t.start()
    i_cross, i_kept = tail_forward(x_v.astype(FLOAT), i_attn, w_cio, w_ciu, w_cid, image_gains[0:2])
    i_low = i_cross.astype(BFLOAT)
    si_packed = project(i_low, w_sip)
    si_attn = self_attend(si_packed, H_V, my_len, False)
    i_final, si_kept = tail_forward(i_cross, si_attn, w_sio, w_siu, w_sid, image_gains[2:4])
    i_res, i_ga, i_pairs, i_gain_s = tail_backward(
        image_cotangent[0].astype(FLOAT), si_kept, si_attn, w_sio, w_siu, w_sid, image_gains[2:4], False
    )
    c1i = Chunk(i_pairs, d_v, halving(0, 2))
    c1i.send, c1i.keep, i_ga, i_res, t_back = close_round(
        [c2t], c1i.send, c1i.keep, i_ga, i_res, t_back
    )

    c2t.start()
    c1i.start()
    si_grads = self_attend_back(si_packed, H_V, my_len, False, i_ga)
    i_back = i_res + mm_t(si_grads, w_sip)
    c2i = Chunk(third_items(si_grads, i_low), d_v, halving(3, 0, 2))
    c2i.send, c2i.keep, i_back, t_back = close_round(
        [c2t, c1i], c2i.send, c2i.keep, i_back, t_back
    )

    for m in (c1i, c2i, c2t):
        m.start()
    t_res, t_ga, t_pairs, t_gain_c = tail_backward(
        t_back, t_kept, t_attn, w_cto, w_ctu, w_ctd, text_gains[0:2], True
    )
    c3a = Chunk(t_pairs[:1], d_t, halving(2, 0))
    c3a.send, c3a.keep, t_res, t_ga, i_back = close_round(
        [c1i, c2i, c2t], c3a.send, c3a.keep, t_res, t_ga, i_back
    )

    for m in (c2i, c1i, c2t, c3a):
        m.start()
    i_res, i_ga, i_pairs, i_gain_c = tail_backward(
        i_back, i_kept, i_attn, w_cio, w_ciu, w_cid, image_gains[0:2], True
    )
    c3b = Whole(t_pairs[1:] + i_pairs, 2 * panel)
    c3b.block, i_res, i_ga, t_ga = close_round([c2i, c1i, c2t, c3a], c3b.block, i_res, i_ga, t_ga)
    c3b.launch()

    for m in (c3a, c2i, c1i, c2t):
        m.start()
    t_grads, i_grads = cross_attend_back(t_packed, i_packed, my_len, t_ga, i_ga)
    t_grads, i_grads = close_round([c3a, c2i, c1i, c2t], t_grads, i_grads)

    for m in (c3a, c2i, c1i):
        m.start()

    def gain_item(products):
        rows = jnp.concatenate(products, axis=0)
        which = jnp.arange(rows.shape[0])[:, None] // products[0].shape[0]
        return whole_item(rows, (which == jnp.arange(panel)[None, :]).astype(BFLOAT))

    c4t = Chunk(third_items(t_grads, x_t) + [gain_item(t_gain_c + t_gain_s)], panel, halving(2, 0))
    c4i = Chunk(third_items(i_grads, x_v) + [gain_item(i_gain_c + i_gain_s)], panel, halving(0, 2))
    c4t.send, c4t.keep, c4i.send, c4i.keep, t_grads, i_grads = close_round(
        [c3a, c2i], c4t.send, c4t.keep, c4i.send, c4i.keep, t_grads, i_grads
    )

    c4t.start()
    c4i.start()
    t_grads, i_grads = close_round([c4t, c4i, c1i], t_grads, i_grads)
    for m in (c4t, c4i, c3a, c2i):
        m.start()
    text_input_grad = t_res + mm_t(t_grads, w_ctp)
    image_input_grad = i_res + mm_t(i_grads, w_cip)
    text_input_grad, image_input_grad, c1t.sum = close_round(
        [c4t, c4i, c3a, c2i], text_input_grad, image_input_grad, c1t.sum
    )
    for m in (c4t, c4i, c3a):
        m.start()
    close_round([c4t, c4i, c3a])
    for last_turn in range(2, bits - 1):
        for m in (c4t, c4i):
            m.start()
        if last_turn == bits - 2:
            (c3b.sum,) = close_round([c4t, c4i], c3b.sum)
        else:
            close_round([c4t, c4i])
    for m in (c1i, c2t, c2i, c3a, c4t, c4i):
        while m.step < bits:
            m.start()
            m.absorb()

    def cut(block, rows):
        out, at = [], 0
        for r in rows:
            out.append(block[at : at + r])
            at += r
        return out

    def widen(block, rows, width):
        wide = block.shape[1]
        return block.reshape(width // wide, rows, wide).transpose(1, 0, 2).reshape(rows, width)

    def thirds(block, rows, width):
        many = rows * (width // panel)
        return jnp.concatenate(
            [widen(block[e * many : (e + 1) * many], rows, width) for e in range(3)], axis=0
        )

    g_std, g_stu, g_sto = cut(c1t.finish(), (ff_t // d_t * own_t, own_f, own_t))
    g_sid, g_siu, g_sio = cut(c1i.full, (own_v,) * 3)
    g_ctd = c3a.full
    kinds = [(own_f, d_t), (own_c, d_t)] + [(own_v, d_v)] * 3
    parts = cut(c3b.finish(), [rows * (width // (2 * panel)) for rows, width in kinds])
    g_ctu, g_cto, g_cid, g_ciu, g_cio = (widen(p, *kind) for p, kind in zip(parts, kinds))
    g_std = g_std.reshape(ff_t // d_t, own_t, d_t).transpose(1, 0, 2).reshape(own_t, ff_t)
    g_stp, g_sip = c2t.full, c2i.full
    g_ctp, g_cip = thirds(c4t.full, own_c, d_t), thirds(c4i.full, own_c, d_v)
    t_gain = c4t.full[-own_t:, :4].T
    i_gain = c4i.full[-own_v:, :4].T

    def by_three(rows):
        return rows.reshape(3, rows.shape[0] // 3, rows.shape[1]).transpose(0, 2, 1)

    o_stu, o_ctu, o_ctd = g_stu.T, g_ctu.T, g_ctd
    o_std, o_sto = g_std.T, g_sto
    o_stp = by_three(g_stp)
    o_sid, o_siu, o_sio = g_sid.T, g_siu.T, g_sio
    o_sip = by_three(g_sip)
    o_cid, o_ciu, o_cio, o_cto = g_cid, g_ciu.T, g_cio, g_cto
    o_cip = by_three(g_cip)
    o_ctp = by_three(g_ctp)
    o_tg, o_ig = t_gain, i_gain
    return (
        t_final.astype(BFLOAT)[None],
        i_final.astype(BFLOAT)[None],
        text_input_grad[None],
        image_input_grad[None],
        o_ctp,
        o_cip,
        o_cto,
        o_cio,
        o_ctu,
        o_ctd,
        o_ciu,
        o_cid,
        o_stp,
        o_sto,
        o_stu,
        o_std,
        o_sip,
        o_sio,
        o_siu,
        o_sid,
        o_tg,
        o_ig,
    )


def solution(mesh):
    row = P(ALL, None)
    batch = P(ALL, None, None)
    col = P(None, ALL)
    proj = P(None, ALL, None)
    proj_grad = P(None, None, ALL)
    in_specs = (batch, batch, P("dp"), batch, batch, proj, proj, row, row, row, row, row, row)
    in_specs += (proj, row, row, row, proj, row, row, row, P(), P())
    out_specs = (batch, batch, batch, batch, proj_grad, proj_grad, row, row, col, row, col, row)
    out_specs += (proj_grad, row, col, col, proj_grad, row, col, col, col, col)
    return jax.shard_map(
        on_device, mesh=mesh, in_specs=in_specs, out_specs=out_specs, check_vma=False
    )
```

```python
import jax
import jax.numpy as jnp
from jax import lax
from jax.experimental import pallas as pl
from jax.experimental.pallas import tpu as pltpu
from jax.sharding import PartitionSpec as P

H_T = 12
H_V = 8
H_C = 8

EPSILON = 1e-05
NEGATIVE = -1000000000.0
FLOAT = jnp.float32
BFLOAT = jnp.bfloat16
ALL = ("dp", "seq")
FREE = pl.CostEstimate(flops=0, bytes_accessed=0, transcendentals=0)


def device_bits():
    return (lax.axis_size("dp").bit_length() - 1, lax.axis_size("seq").bit_length() - 1)


def my_index():
    return lax.axis_index("dp") * lax.axis_size("seq") + lax.axis_index("seq")


def swap(block, bit):
    size = lax.axis_size("dp") * lax.axis_size("seq")
    return lax.ppermute(block, ALL, [(i, i ^ (1 << bit)) for i in range(size)])


def orders():
    dp_bits, seq_bits = device_bits()
    total = dp_bits + seq_bits
    core = seq_bits
    rest = [b for b in range(total) if b != core]
    seq_first = [core] + rest
    dp_first = [core] + rest[1:2] + rest[0:1] + rest[2:]
    far_first = [core] + rest[2:3] + rest[1:2] + rest[0:1] + rest[3:]
    return seq_first, dp_first, far_first


def take(block, which):
    return lax.dynamic_index_in_dim(block, which, 0, keepdims=False)


def add_low(left, right):
    return (left.astype(FLOAT) + right.astype(FLOAT)).astype(BFLOAT)


def join_blocks(held, came, order, splits):
    count, rows, width = held.shape
    bits = len(order)
    near = order.index(0)
    low = 1 << near
    pairs = (count // (2 * low), 2, low, rows, width)

    def out_index(j, at):
        place = jnp.int32(0)
        for k, b in enumerate(order[:-1]):
            if b != 0:
                bit = lax.rem(lax.shift_right_logical(j, k if k < near else k - 1), 2)
                place = place + lax.shift_left(bit, b)
        block = jnp.bitwise_xor(at[0], place)
        return (lax.shift_right_logical(block, 2), 0, 0, 0, 0)

    def body(at_ref, held_ref, came_ref, *outs):
        side = lax.rem(lax.shift_right_logical(at_ref[0], 1), 2)
        mine = lax.rem(at_ref[0], 2)
        start = 0
        for out, many in zip(outs, splits):
            for step in range(2):
                y = jnp.bitwise_xor(mine, step)
                out[0, side, y] = held_ref[0, step, 0, start : start + many]
                out[0, 1 - side, y] = came_ref[0, step, 0, start : start + many]
            start += many

    def in_index(j, at):
        return (lax.div(j, low), 0, lax.rem(j, low), 0, 0)

    outs = pl.pallas_call(
        body,
        grid_spec=pltpu.PrefetchScalarGridSpec(
            num_scalar_prefetch=1,
            grid=(count // 2,),
            in_specs=[pl.BlockSpec((1, 2, 1, rows, width), in_index)] * 2,
            out_specs=[pl.BlockSpec((1, 2, 2, many, width), out_index) for many in splits],
        ),
        out_shape=[
            jax.ShapeDtypeStruct((1 << (bits - 2), 2, 2, many, width), held.dtype) for many in splits
        ],
        compiler_params=pltpu.CompilerParams(vmem_limit_bytes=32 * 1024 * 1024),
        cost_estimate=FREE,
    )(my_index().astype(jnp.int32).reshape(1), held.reshape(pairs), came.reshape(pairs))
    return [out.reshape(-1, width) for out in outs]


class Gather:
    def __init__(self, shard, order, splits=None):
        self.order = order
        self.send = shard[None]
        self.splits = splits or [shard.shape[0]]
        self.step = 0

    def start(self):
        self.came = swap(self.send, self.order[self.step])
        self.step += 1

    def absorb(self):
        if self.step == len(self.order):
            self.full = join_blocks(self.send, self.came, self.order, self.splits)
        else:
            self.send = jnp.concatenate([self.send, self.came], axis=0)


def close_round(movers, *arrays):
    came = [m.came for m in movers]
    came, arrays = lax.optimization_barrier((came, arrays))
    for m, block in zip(movers, came):
        m.came = block
    for m in movers:
        m.absorb()
    going = [m for m in movers if m.step < len(m.order)]
    sends, arrays = lax.optimization_barrier(([m.send for m in going], arrays))
    for m, block in zip(going, sends):
        m.send = block
    return arrays


def sides_of(order):
    at = my_index()
    return [lax.rem(lax.shift_right_logical(at, b), 2) for b in order]


def panels_of(other, width):
    return other.shape[1] // width


def rows_in_order(rows, first, own, size, order):
    total = len(order)
    part = rows[:, first : first + own * size]
    split = part.reshape((part.shape[0],) + (2,) * total + (own,))
    axes = [1 + (total - 1 - b) for b in order] + [1 + total, 0]
    return split.transpose(axes).reshape(size * own, part.shape[0])


def pack_plain(items, width, order):
    size = 1 << len(order)
    parts = []
    for rows, first, span, other in items:
        own = span // size
        block = mm(rows_in_order(rows, first, own, size, order), other).astype(BFLOAT)
        block = block.reshape(size, own, panels_of(other, width), width).transpose(0, 2, 1, 3)
        parts.append(block.reshape(size, -1, width))
    return jnp.concatenate(parts, axis=1)


def pack_kernel(items, width, order, natural):
    total = len(order)
    size = 1 << total
    groups = size // 4
    core_side = sides_of(order[:1])[0]
    owns = [span // size for rows, first, span, other in items]
    panels = [panels_of(other, width) for rows, first, span, other in items]
    count = len(items)
    total_rows = sum(o * p for o, p in zip(owns, panels))
    lefts, left_specs = [], []
    for (rows, first, span, other), own in zip(items, owns):
        length = rows.shape[0]
        at = first // (4 * own)
        if (4 * own) % 128 == 0:
            lefts.append(rows)
            left_specs.append(pl.BlockSpec((length, 4 * own), lambda g, core, at=at: (0, at + g)))
        else:
            lefts.append(rows.reshape(length, -1, 4 * own).transpose(1, 0, 2))
            left_specs.append(pl.BlockSpec((None, length, 4 * own), lambda g, core, at=at: (at + g, 0, 0)))
    rights, used = [], []
    for item in items:
        match = [i for i, other in enumerate(rights) if other is item[3]]
        if not match:
            rights.append(item[3])
        used.append(match[0] if match else len(rights) - 1)
    right_specs = [pl.BlockSpec(other.shape, lambda g, core: (0, 0)) for other in rights]
    rest = order[1:]

    def out_index(g, core):
        return tuple(0 if b == 0 else lax.rem(lax.shift_right_logical(g, b - 2), 2) for b in rest) + (0, 0)

    out_shape = (2,) * len(rest) + (total_rows, width)
    out_block = tuple(2 if b == 0 else None for b in rest) + (total_rows, width)
    outs = 1 if natural else 2
    if natural:
        out_shape = (size, total_rows, width)
        out_block = (4, total_rows, width)
        out_index = lambda g, core: (g, 0, 0)

    def body(core_ref, *refs):
        left_refs = refs[:count]
        right_refs = refs[count : count + len(rights)]
        pack_refs = refs[count + len(rights) : count + len(rights) + outs]
        held = refs[count + len(rights) + outs :]
        core = core_ref[0]
        for left, right, keepers in zip(left_refs, used, held):
            keepers[...] = t_mm(left[...], right_refs[right][...])
        if natural:
            targets = [(pack_refs[0], i, i) for i in range(4)]
        else:
            targets = [(pack_refs[0], i, 2 * (1 - core) + i) for i in range(2)]
            targets += [(pack_refs[1], i, 2 * core + i) for i in range(2)]
        for ref, near, which in targets:
            pieces = []
            for keepers, own, many in zip(held, owns, panels):
                start = which * own if natural else pl.multiple_of(which * own, 8)
                for p in range(many):
                    pieces.append(keepers[pl.ds(start, own), p * width : (p + 1) * width])
            ref[near] = jnp.concatenate(pieces, axis=0).astype(BFLOAT)

    flops = sum(2 * rows.shape[0] * span * other.shape[1] for rows, first, span, other in items)
    packed = pl.pallas_call(
        body,
        grid_spec=pltpu.PrefetchScalarGridSpec(
            num_scalar_prefetch=1,
            grid=(groups,),
            in_specs=left_specs + right_specs,
            out_specs=[pl.BlockSpec(out_block, out_index)] * outs,
            scratch_shapes=[
                pltpu.VMEM((4 * own, other.shape[1]), FLOAT)
                for own, (rows, first, span, other) in zip(owns, items)
            ],
        ),
        out_shape=[jax.ShapeDtypeStruct(out_shape, BFLOAT)] * outs,
        compiler_params=pltpu.CompilerParams(vmem_limit_bytes=32 * 1024 * 1024),
        cost_estimate=FREE,
    )(core_side.astype(jnp.int32).reshape(1), *lefts, *rights)
    if natural:
        return packed[0]
    flat = (size // 2, total_rows, width)
    return packed[0].reshape(flat), packed[1].reshape(flat)


def aligned_items(items, size):
    return all(span % (8 * size) == 0 for rows, first, span, other in items)


def pack_natural(items, width):
    bits = sum(device_bits())
    if aligned_items(items, 1 << bits):
        return pack_kernel(items, width, list(range(bits)), True)
    return pack_plain(items, width, list(range(bits))[::-1])


def pack(items, width, order):
    size = 1 << len(order)
    if aligned_items(items, size) and order[0] == 1:
        return pack_kernel(items, width, order, False)
    block = pack_plain(items, width, order)
    block = block.reshape((2, size // 2) + block.shape[1:])
    at = sides_of(order[:1])[0]
    return take(block, 1 - at), take(block, at)


class Whole:
    def __init__(self, items, width):
        self.block = pack_natural(items, width)

    def launch(self):
        flat = self.block.reshape(-1, self.block.shape[-1])
        self.sum = lax.psum_scatter(flat, ALL, scatter_dimension=0, tiled=True)

    def finish(self):
        return self.sum.astype(FLOAT)


class Chunk:
    def __init__(self, items, width, order):
        self.order = order
        self.sides = sides_of(order)
        self.send, self.keep = pack(items, width, order)
        self.step = 0

    def start(self):
        self.came = swap(self.send, self.order[self.step])
        self.step += 1

    def absorb(self):
        if self.step == len(self.order):
            self.full = (self.came.astype(FLOAT) + self.keep.astype(FLOAT))[0]
            return
        half = self.came.shape[0] // 2
        came = self.came.reshape((2, half) + self.came.shape[1:])
        keep = self.keep.reshape((2, half) + self.keep.shape[1:])
        at = self.sides[self.step]
        self.send = add_low(take(came, 1 - at), take(keep, 1 - at))
        self.keep = add_low(take(came, at), take(keep, at))


class Small(Chunk):
    def __init__(self, block, order):
        total = len(order)
        tail = block.shape[1:]
        held = block.reshape((2,) * total + tail)
        held = held.transpose([total - 1 - b for b in order] + [total + i for i in range(len(tail))])
        held = held.reshape((2, -1) + tail)
        self.order = order
        self.sides = sides_of(order)
        self.send, self.keep = take(held, 1 - self.sides[0]), take(held, self.sides[0])
        self.step = 0


def mm(left, right):
    return jnp.dot(left, right, preferred_element_type=FLOAT)


def mm_t(left, right):
    return lax.dot_general(left, right, (((1,), (1,)), ((), ())), preferred_element_type=FLOAT)


def t_mm(left, right):
    return lax.dot_general(left, right, (((0,), (0,)), ((), ())), preferred_element_type=FLOAT)


def layer_norm(stream, gain_vec):
    center = stream - jnp.mean(stream, axis=-1, keepdims=True)
    spread = jnp.mean(center * center, axis=-1, keepdims=True)
    return center * lax.rsqrt(spread + EPSILON) * gain_vec


def norm_back(stream, gain_vec, upstream):
    center = stream - jnp.mean(stream, axis=-1, keepdims=True)
    scale = lax.rsqrt(jnp.mean(center * center, axis=-1, keepdims=True) + EPSILON)
    unit = center * scale
    weighted = upstream * gain_vec
    inner = jnp.mean(weighted * unit, axis=-1, keepdims=True)
    grad = (weighted - jnp.mean(weighted, axis=-1, keepdims=True) - unit * inner) * scale
    return grad, jnp.sum(upstream * unit, axis=0)


def gelu_back(upper, upstream):
    unused, pullback = jax.vjp(jax.nn.gelu, upper)
    return pullback(upstream)[0]


def head_blocks(width, heads):
    size = width // heads
    block = max(size, 128)
    return [(h * size // block * block, block, h * size % block, size) for h in range(heads)]


def only_head(value, start, size):
    if size == value.shape[1]:
        return value
    lane = lax.broadcasted_iota(jnp.int32, value.shape, 1)
    return jnp.where((lane >= start) & (lane < start + size), value, jnp.zeros_like(value))


def head_probs(query, key, size, valid):
    scores = mm_t(query, key) * (size ** (-0.5))
    if valid is not None:
        lane = lax.broadcasted_iota(jnp.int32, scores.shape, 1)
        scores = jnp.where(lane < valid, scores, NEGATIVE)
    expo = jnp.exp(scores - jnp.max(scores, axis=-1, keepdims=True))
    return expo / jnp.sum(expo, axis=-1, keepdims=True)


def attend_block(q_ref, k_ref, v_ref, q_at, k_at, v_at, out_ref, heads, valid):
    width = out_ref.shape[1]
    parts = {}
    for base, block, start, size in head_blocks(width, heads):
        q = only_head(q_ref[:, q_at + base : q_at + base + block], start, size)
        k = k_ref[:, k_at + base : k_at + base + block]
        v = only_head(v_ref[:, v_at + base : v_at + base + block], start, size)
        part = mm(head_probs(q, k, size, valid).astype(BFLOAT), v)
        parts[base] = part if base not in parts else parts[base] + part
        if start + size == block:
            out_ref[:, base : base + block] = parts[base].astype(BFLOAT)


def attend_block_back(
    q_ref, k_ref, v_ref, q_at, k_at, v_at, g_ref, dq_ref, dk_ref, dv_ref, heads, valid
):
    width = g_ref.shape[1]
    parts = {}
    for base, block, start, size in head_blocks(width, heads):
        q = only_head(q_ref[:, q_at + base : q_at + base + block], start, size)
        k = only_head(k_ref[:, k_at + base : k_at + base + block], start, size)
        v = v_ref[:, v_at + base : v_at + base + block]
        g = only_head(g_ref[:, base : base + block], start, size)
        probs = head_probs(q, k, size, valid)
        grad_probs = mm_t(g, v)
        inner = jnp.sum(grad_probs * probs, axis=-1, keepdims=True)
        grad_scores = (probs * (grad_probs - inner)).astype(BFLOAT)
        scale = size ** (-0.5)
        news = (mm(grad_scores, k) * scale, t_mm(grad_scores, q) * scale, t_mm(probs.astype(BFLOAT), g))
        if base in parts:
            news = tuple(x + y for x, y in zip(parts[base], news))
        parts[base] = news
        if start + size == block:
            for ref, at, new in zip((dq_ref, dk_ref, dv_ref), (q_at, k_at, v_at), news):
                ref[:, at + base : at + base + block] = new.astype(BFLOAT)


def vmem_call(body, count, outs, scalar, flops, *operands):
    return pl.pallas_call(
        body,
        in_specs=[pl.BlockSpec(memory_space=pltpu.SMEM)] + [pl.BlockSpec(memory_space=pltpu.VMEM)] * count,
        out_specs=[pl.BlockSpec(memory_space=pltpu.VMEM)] * len(outs),
        out_shape=[jax.ShapeDtypeStruct(shape, BFLOAT) for shape in outs],
        compiler_params=pltpu.CompilerParams(vmem_limit_bytes=32 * 1024 * 1024),
        cost_estimate=FREE,
    )(scalar, *operands)


def cross_attend(text, image, length):
    width = text.shape[1] // 3

    def body(len_ref, text_ref, image_ref, t_ref, i_ref):
        attend_block(text_ref, image_ref, image_ref, 0, width, 2 * width, t_ref, H_C, None)
        attend_block(image_ref, text_ref, text_ref, 0, width, 2 * width, i_ref, H_C, len_ref[0])

    flops = 8 * text.shape[0] * image.shape[0] * width * 8
    outs = [(text.shape[0], width), (image.shape[0], width)]
    return vmem_call(body, 2, outs, length, flops, text, image)


def cross_attend_back(text, image, length, t_grad, i_grad):
    width = text.shape[1] // 3

    def body(len_ref, text_ref, image_ref, tg_ref, ig_ref, dt_ref, di_ref):
        attend_block_back(
            text_ref, image_ref, image_ref, 0, width, 2 * width, tg_ref, dt_ref, di_ref, di_ref, H_C, None
        )
        attend_block_back(
            image_ref, text_ref, text_ref, 0, width, 2 * width, ig_ref, di_ref, dt_ref, dt_ref, H_C, len_ref[0]
        )

    flops = 20 * text.shape[0] * image.shape[0] * width * 8
    return vmem_call(body, 4, [text.shape, image.shape], length, flops, text, image, t_grad, i_grad)


def self_attend(packed, heads, length, masked):
    width = packed.shape[1] // 3

    def body(len_ref, ref, out_ref):
        attend_block(ref, ref, ref, 0, width, 2 * width, out_ref, heads, len_ref[0] if masked else None)

    flops = 4 * packed.shape[0] * packed.shape[0] * width * 8
    return vmem_call(body, 1, [(packed.shape[0], width)], length, flops, packed)[0]


def self_attend_back(packed, heads, length, masked, grad):
    width = packed.shape[1] // 3

    def body(len_ref, ref, g_ref, d_ref):
        attend_block_back(
            ref, ref, ref, 0, width, 2 * width, g_ref, d_ref, d_ref, d_ref, heads, len_ref[0] if masked else None
        )

    flops = 10 * packed.shape[0] * packed.shape[0] * width * 8
    return vmem_call(body, 2, [packed.shape], length, flops, packed, grad)[0]


def tail_forward(residual, attn_low, out_mat, up_mat, down_mat, gain_pair):
    first_sum = residual + mm(attn_low, out_mat)
    first_norm = layer_norm(first_sum, gain_pair[0])
    hidden_low = first_norm.astype(BFLOAT)
    upper = mm(hidden_low, up_mat)
    active = jax.nn.gelu(upper).astype(BFLOAT)
    second_sum = first_norm + mm(active, down_mat)
    return layer_norm(second_sum, gain_pair[1]), (first_sum, hidden_low, upper, active, second_sum)


def tail_backward(grad_result, kept, attn_low, out_mat, up_mat, down_mat, gain_pair, down_natural):
    first_sum, hidden_low, upper, active, second_sum = kept
    grad_second, gain_two = norm_back(second_sum, gain_pair[1], grad_result)
    low = grad_second.astype(BFLOAT)
    grad_down = whole_item(active, low) if down_natural else whole_item(low, active)
    grad_upper = gelu_back(upper, mm_t(low, down_mat)).astype(BFLOAT)
    grad_up = whole_item(grad_upper, hidden_low)
    grad_norm = grad_second + mm_t(grad_upper, up_mat)
    grad_first, gain_one = norm_back(first_sum, gain_pair[0], grad_norm)
    grad_first_low = grad_first.astype(BFLOAT)
    grad_out = whole_item(attn_low, grad_first_low)
    grad_attn = mm_t(grad_first_low, out_mat).astype(BFLOAT)
    return grad_first, grad_attn, [grad_down, grad_up, grad_out], [gain_one, gain_two]


def project(stream_low, proj):
    return mm(stream_low, proj).astype(BFLOAT)


def whole_item(rows, other):
    return (rows, 0, rows.shape[1], other)


def third_items(packed, other):
    span = packed.shape[1] // 3
    return [(packed, e * span, span, other) for e in range(3)]


def side(shards):
    return jnp.concatenate(shards, axis=1)


def on_device(
    text_input,
    image_input,
    caption_lengths,
    text_cotangent,
    image_cotangent,
    cross_text_proj,
    cross_image_proj,
    cross_text_out,
    cross_image_out,
    cross_text_up,
    cross_text_down,
    cross_image_up,
    cross_image_down,
    self_text_proj,
    self_text_out,
    self_text_up,
    self_text_down,
    self_image_proj,
    self_image_out,
    self_image_up,
    self_image_down,
    text_gains,
    image_gains,
):
    d_t = text_input.shape[2]
    d_v = image_input.shape[2]
    co = cross_text_proj.shape[2]
    ff_t = cross_text_up.shape[1]
    n_text = text_input.shape[1]

    size = lax.axis_size("dp") * lax.axis_size("seq")
    bits = sum(device_bits())
    by_permute = size == 1 << bits and all(
        m.shape[-2] % 8 == 0 for m in (cross_text_out, cross_text_down, self_text_down)
    )

    def gather_columns(parts):
        return lax.all_gather(side(parts), ALL, axis=0, tiled=True)

    own_t, own_v = d_t // size, d_v // size
    own_f, own_c = ff_t // size, co // size
    text_parts = list(cross_text_proj) + [cross_text_up] + list(self_text_proj)
    text_wide = gather_columns(text_parts + [self_text_out, self_text_up])
    image_parts = [cross_image_out, cross_image_up, cross_image_down] + list(self_image_proj)
    image_wide = gather_columns(image_parts + [self_image_out, self_image_up, self_image_down])
    w_ctp = text_wide[:, : 3 * co]

    high = list(range(3, bits))[::-1]
    x_first = high + [2, 0, 1]
    y_first = high + [0, 2, 1]
    shards = [
        (side(list(cross_image_proj)), y_first, None),
        (jnp.concatenate([cross_text_down, cross_text_out], axis=0), x_first, [own_f, own_c]),
        (self_text_down, x_first, None),
    ]

    panel = 128
    my_len = lax.dynamic_index_in_dim(caption_lengths, lax.axis_index("seq"), 0, keepdims=True)
    x_t = text_input[0]
    x_v = image_input[0]

    if by_permute:
        movers = [Gather(*item) for item in shards]
        for turn_at in range(bits):
            active = movers[:2] + ([movers[2]] if turn_at >= 2 else [])
            for m in active:
                m.start()
            close_round(active)
        w_cip = movers[0].full[0]
        w_ctd, w_cto = movers[1].full
        movers[2].start()
        t_packed = project(x_t, w_ctp)
        i_packed = project(x_v, w_cip)
        t_attn, i_attn = cross_attend(t_packed, i_packed, my_len)
        t_attn, i_attn = close_round(movers[2:], t_attn, i_attn)
        movers[2].start()
    else:
        full = [lax.all_gather(shard, ALL, axis=0) for shard, order, splits in shards]
        w_ctd, w_cto = full[1][:, :own_f], full[1][:, own_f:]
        w_cip, w_ctd, w_cto, w_std = (w.reshape(-1, w.shape[-1]) for w in (full[0], w_ctd, w_cto, full[2]))
        t_packed = project(x_t, w_ctp)
        i_packed = project(x_v, w_cip)
        t_attn, i_attn = cross_attend(t_packed, i_packed, my_len)

    w_ctu = text_wide[:, 3 * co : 3 * co + ff_t]
    text_self = text_wide[:, 3 * co + ff_t :]
    w_stp, w_sto, w_stu = text_self[:, : 3 * d_t], text_self[:, 3 * d_t : 4 * d_t], text_self[:, 4 * d_t :]

    def halving(*picks):
        return [1] + list(picks) + [b for b in range(bits) if b != 1 and b not in picks]

    t_cross, t_kept = tail_forward(x_t.astype(FLOAT), t_attn, w_cto, w_ctu, w_ctd, text_gains[0:2])
    t_low = t_cross.astype(BFLOAT)
    if by_permute:
        t_cross, t_kept = close_round(movers[2:], t_cross, t_kept)
        w_std = movers[2].full[0]
        t_low = t_cross.astype(BFLOAT)
    st_packed = project(t_low, w_stp)
    st_attn = self_attend(st_packed, H_T, my_len, True)
    t_final, st_kept = tail_forward(t_cross, st_attn, w_sto, w_stu, w_std, text_gains[2:4])
    t_res, t_ga, t_pairs, t_gain_s = tail_backward(
        text_cotangent[0].astype(FLOAT), st_kept, st_attn, w_sto, w_stu, w_std, text_gains[2:4], False
    )
    def start(*movers):
        for m in movers:
            if m.step < bits:
                m.start()

    def by_owner(packed, own):
        rows = packed.shape[0]
        blocks = packed.reshape(rows, 3, size, own).transpose(2, 0, 1, 3).reshape(size, rows, 3 * own)
        return jnp.pad(blocks, ((0, 0), (0, -rows % 8), (0, 3 * (own_v - own))))

    def exchange(*blocks):
        return lax.all_to_all(
            jnp.concatenate(blocks, axis=1), ALL, split_axis=0, concat_axis=0, tiled=True
        )

    c1a = Chunk(t_pairs[:1], d_t, halving(2, 0))
    c1b = Chunk(t_pairs[1:], d_t, halving(0, 2))
    t_ga, t_res, i_attn = close_round([], t_ga, t_res, i_attn)

    start(c1a, c1b)
    st_grads = self_attend_back(st_packed, H_T, my_len, True, t_ga)
    t_back = t_res + mm_t(st_grads, w_stp)
    st_grads, t_back, i_attn = close_round([c1a, c1b], st_grads, t_back, i_attn)

    start(c1a, c1b)
    t_res, t_ga, t_pairs, t_gain_c = tail_backward(
        t_back, t_kept, t_attn, w_cto, w_ctu, w_ctd, text_gains[0:2], True
    )
    c3a = Chunk([t_pairs[0], t_pairs[2]], d_t, halving(2, 0))
    c3b = Chunk(t_pairs[1:2], d_t, halving(0, 2))
    c3a.send, c3a.keep, c3b.send, c3b.keep, t_res, t_ga, i_attn = close_round(
        [c1a, c1b], c3a.send, c3a.keep, c3b.send, c3b.keep, t_res, t_ga, i_attn
    )
    start(c1a, c1b, c3a, c3b)
    (i_attn,) = close_round([c1a, c1b, c3a, c3b], i_attn)

    w_cio, w_ciu, w_cid = (image_wide[:, i * d_v : (i + 1) * d_v] for i in range(3))
    w_sip = image_wide[:, 3 * d_v : 6 * d_v]
    w_sio, w_siu, w_sid = (image_wide[:, (6 + i) * d_v : (7 + i) * d_v] for i in range(3))

    start(c3a, c3b, c1a, c1b)
    i_cross, i_kept = tail_forward(x_v.astype(FLOAT), i_attn, w_cio, w_ciu, w_cid, image_gains[0:2])
    i_low = i_cross.astype(BFLOAT)
    if by_permute:
        tall = -(-x_t.shape[0] // 8) * 8
        seen = [x_v.reshape(-1, d_t), i_low.reshape(-1, d_t)]
        seen += [jnp.pad(m, ((0, tall - m.shape[0]), (0, 0))) for m in (x_t, t_low)]
        seen = jnp.concatenate(seen, axis=0)
    si_packed = project(i_low, w_sip)
    si_attn = self_attend(si_packed, H_V, my_len, False)
    i_final, si_kept = tail_forward(i_cross, si_attn, w_sio, w_siu, w_sid, image_gains[2:4])
    i_res, i_ga, i_pairs, i_gain_s = tail_backward(
        image_cotangent[0].astype(FLOAT), si_kept, si_attn, w_sio, w_siu, w_sid, image_gains[2:4], False
    )
    c1i = Chunk(i_pairs, d_v, halving(0, 2))
    c1i.send, c1i.keep, i_ga, i_res = close_round(
        [c1a, c1b, c3a, c3b], c1i.send, c1i.keep, i_ga, i_res
    )
    if by_permute:
        seen = lax.all_gather(seen, ALL, axis=0)

    start(c1i, c3a, c3b)
    si_grads = self_attend_back(si_packed, H_V, my_len, False, i_ga)
    i_back = i_res + mm_t(si_grads, w_sip)
    si_grads, i_back = close_round([c1i, c3a, c3b], si_grads, i_back)
    self_slices = t_low
    if by_permute:
        self_slices = exchange(by_owner(st_grads, own_t), by_owner(si_grads, own_v))

    start(c1i, c3a, c3b)
    i_res, i_ga, i_pairs, i_gain_c = tail_backward(
        i_back, i_kept, i_attn, w_cio, w_ciu, w_cid, image_gains[0:2], True
    )
    c3x = Chunk(i_pairs[:1], d_v, halving(2, 0))
    c3y = Chunk(i_pairs[1:], d_v, halving(0, 2))
    c3x.send, c3x.keep, c3y.send, c3y.keep, i_res, i_ga, t_ga, self_slices = close_round(
        [c1i, c3a, c3b], c3x.send, c3x.keep, c3y.send, c3y.keep, i_res, i_ga, t_ga, self_slices
    )

    start(c3x, c3y, c1i)
    t_grads, i_grads = cross_attend_back(t_packed, i_packed, my_len, t_ga, i_ga)
    t_grads, i_grads = close_round([c3x, c3y, c1i], t_grads, i_grads)

    t_gain = jnp.stack(t_gain_c + t_gain_s)
    i_gain = jnp.stack(i_gain_c + i_gain_s)
    start(c3x, c3y, c1i)
    if by_permute:
        gain_rows = [t_gain.reshape(4, size, own_t), i_gain.reshape(4, size, own_v)]
        gain_rows = [
            jnp.pad(g.astype(BFLOAT), ((0, 0), (0, 0), (0, 3 * own_v - g.shape[2]))) for g in gain_rows
        ]
        gain_rows = jnp.concatenate(gain_rows, axis=0).transpose(1, 0, 2)
        cross_slices = exchange(by_owner(t_grads, own_c), by_owner(i_grads, own_c), gain_rows)
    close_round([c3x, c3y, c1i])
    start(c3x, c3y, c1i)
    text_input_grad = t_res + mm_t(t_grads, w_ctp)
    image_input_grad = i_res + mm_t(i_grads, w_cip)
    text_input_grad, image_input_grad = close_round([c3x, c3y, c1i], text_input_grad, image_input_grad)
    start(c3x, c3y, c3a, c3b)
    close_round([c3x, c3y, c3a, c3b])
    start(c3x, c3y, c1a, c1b)
    close_round([c3x, c3y, c1a, c1b])
    for m in (c1a, c1b, c3a, c3b, c1i, c3x, c3y):
        while m.step < bits:
            m.start()
            m.absorb()

    def slices_grad(rows, slices, own):
        grad = t_mm(rows, slices)[:, : 3 * own]
        return grad.reshape(grad.shape[0], 3, own).transpose(1, 0, 2)

    if by_permute:
        short = x_v.size // d_t
        wide_v = x_v.shape[0]
        tall_v = -(-wide_v // 8) * 8

        def rows_of(at, rows):
            return seen[:, at : at + rows]

        def flat_slices(slices, at, rows):
            return slices[:, at : at + rows].reshape(-1, slices.shape[2])

        all_v = rows_of(0, short).reshape(-1, d_v)
        all_low_v = rows_of(short, short).reshape(-1, d_v)
        all_t = rows_of(2 * short, tall).reshape(-1, d_t)
        all_low_t = rows_of(2 * short + tall, tall).reshape(-1, d_t)
        o_stp = slices_grad(all_low_t, flat_slices(self_slices, 0, tall), own_t)
        o_sip = slices_grad(all_low_v, flat_slices(self_slices, tall, wide_v), own_v)
        o_ctp = slices_grad(all_t, flat_slices(cross_slices, 0, tall), own_c)
        o_cip = slices_grad(all_v, flat_slices(cross_slices, tall, wide_v), own_c)
        gain_sum = jnp.sum(cross_slices[:, tall + tall_v :].astype(FLOAT), axis=0)
        o_tg, o_ig = gain_sum[:4, :own_t], gain_sum[4:, :own_v]
    else:

        def by_scatter(packed, rows):
            whole = Whole(third_items(packed, rows), rows.shape[1])
            whole.launch()
            block = whole.finish()
            return block.reshape(3, block.shape[0] // 3, block.shape[1]).transpose(0, 2, 1)

        o_stp, o_sip = by_scatter(st_grads, t_low), by_scatter(si_grads, i_low)
        o_ctp, o_cip = by_scatter(t_grads, x_t), by_scatter(i_grads, x_v)
        at = my_index()
        t_gain, i_gain = lax.psum(t_gain, ALL), lax.psum(i_gain, ALL)
        o_tg = lax.dynamic_slice_in_dim(t_gain, at * own_t, own_t, 1)
        o_ig = lax.dynamic_slice_in_dim(i_gain, at * own_v, own_v, 1)

    def cut(block, rows):
        out, at = [], 0
        for r in rows:
            out.append(block[at : at + r])
            at += r
        return out

    (g_std,) = cut(c1a.full, (ff_t // d_t * own_t,))
    g_stu, g_sto = cut(c1b.full, (own_f, own_t))
    g_sid, g_siu, g_sio = cut(c1i.full, (own_v,) * 3)
    g_ctd, g_cto = cut(c3a.full, (own_f, own_c))
    g_ctu, g_cid = c3b.full, c3x.full
    g_ciu, g_cio = cut(c3y.full, (own_v,) * 2)
    g_std = g_std.reshape(ff_t // d_t, own_t, d_t).transpose(1, 0, 2).reshape(own_t, ff_t)

    o_stu, o_ctu, o_ctd = g_stu.T, g_ctu.T, g_ctd
    o_std, o_sto = g_std.T, g_sto
    o_sid, o_siu, o_sio = g_sid.T, g_siu.T, g_sio
    o_cid, o_ciu, o_cio, o_cto = g_cid, g_ciu.T, g_cio, g_cto
    return (
        t_final.astype(BFLOAT)[None],
        i_final.astype(BFLOAT)[None],
        text_input_grad[None],
        image_input_grad[None],
        o_ctp,
        o_cip,
        o_cto,
        o_cio,
        o_ctu,
        o_ctd,
        o_ciu,
        o_cid,
        o_stp,
        o_sto,
        o_stu,
        o_std,
        o_sip,
        o_sio,
        o_siu,
        o_sid,
        o_tg,
        o_ig,
    )


def solution(mesh):
    row = P(ALL, None)
    batch = P(ALL, None, None)
    col = P(None, ALL)
    proj = P(None, ALL, None)
    proj_grad = P(None, None, ALL)
    in_specs = (batch, batch, P("dp"), batch, batch, proj, proj, row, row, row, row, row, row)
    in_specs += (proj, row, row, row, proj, row, row, row, P(), P())
    out_specs = (batch, batch, batch, batch, proj_grad, proj_grad, row, row, col, row, col, row)
    out_specs += (proj_grad, row, col, col, proj_grad, row, col, col, col, col)
    return jax.shard_map(
        on_device, mesh=mesh, in_specs=in_specs, out_specs=out_specs, check_vma=False
    )
```

```python
import jax
import jax.numpy as jnp
from jax import lax
from jax.experimental import pallas as pl
from jax.experimental.pallas import tpu as pltpu
from jax.sharding import PartitionSpec as P

H_T = 12
H_V = 8
H_C = 8

EPSILON = 1e-05
NEGATIVE = -1000000000.0
FLOAT = jnp.float32
BFLOAT = jnp.bfloat16
ALL = ("dp", "seq")
FREE = pl.CostEstimate(flops=0, bytes_accessed=0, transcendentals=0)


def device_bits():
    return (lax.axis_size("dp").bit_length() - 1, lax.axis_size("seq").bit_length() - 1)


def my_index():
    return lax.axis_index("dp") * lax.axis_size("seq") + lax.axis_index("seq")


def swap(block, bit):
    size = lax.axis_size("dp") * lax.axis_size("seq")
    return lax.ppermute(block, ALL, [(i, i ^ (1 << bit)) for i in range(size)])


def orders():
    dp_bits, seq_bits = device_bits()
    total = dp_bits + seq_bits
    core = seq_bits
    rest = [b for b in range(total) if b != core]
    seq_first = [core] + rest
    dp_first = [core] + rest[1:2] + rest[0:1] + rest[2:]
    far_first = [core] + rest[2:3] + rest[1:2] + rest[0:1] + rest[3:]
    return seq_first, dp_first, far_first


def take(block, which):
    return lax.dynamic_index_in_dim(block, which, 0, keepdims=False)


def add_low(left, right):
    return (left.astype(FLOAT) + right.astype(FLOAT)).astype(BFLOAT)


def join_blocks(held, came, order, splits):
    count, rows, width = held.shape
    bits = len(order)
    near = order.index(0)
    low = 1 << near
    pairs = (count // (2 * low), 2, low, rows, width)

    def out_index(j, at):
        place = jnp.int32(0)
        for k, b in enumerate(order[:-1]):
            if b != 0:
                bit = lax.rem(lax.shift_right_logical(j, k if k < near else k - 1), 2)
                place = place + lax.shift_left(bit, b)
        block = jnp.bitwise_xor(at[0], place)
        return (lax.shift_right_logical(block, 2), 0, 0, 0, 0)

    def body(at_ref, held_ref, came_ref, *outs):
        side = lax.rem(lax.shift_right_logical(at_ref[0], 1), 2)
        mine = lax.rem(at_ref[0], 2)
        start = 0
        for out, many in zip(outs, splits):
            for step in range(2):
                y = jnp.bitwise_xor(mine, step)
                out[0, side, y] = held_ref[0, step, 0, start : start + many]
                out[0, 1 - side, y] = came_ref[0, step, 0, start : start + many]
            start += many

    def in_index(j, at):
        return (lax.div(j, low), 0, lax.rem(j, low), 0, 0)

    outs = pl.pallas_call(
        body,
        grid_spec=pltpu.PrefetchScalarGridSpec(
            num_scalar_prefetch=1,
            grid=(count // 2,),
            in_specs=[pl.BlockSpec((1, 2, 1, rows, width), in_index)] * 2,
            out_specs=[pl.BlockSpec((1, 2, 2, many, width), out_index) for many in splits],
        ),
        out_shape=[
            jax.ShapeDtypeStruct((1 << (bits - 2), 2, 2, many, width), held.dtype) for many in splits
        ],
        compiler_params=pltpu.CompilerParams(vmem_limit_bytes=32 * 1024 * 1024),
        cost_estimate=FREE,
    )(my_index().astype(jnp.int32).reshape(1), held.reshape(pairs), came.reshape(pairs))
    return [out.reshape(-1, width) for out in outs]


class Gather:
    def __init__(self, shard, order, splits=None):
        self.order = order
        self.send = shard[None]
        self.splits = splits or [shard.shape[0]]
        self.step = 0

    def start(self):
        self.came = swap(self.send, self.order[self.step])
        self.step += 1

    def absorb(self):
        if self.step == len(self.order):
            self.full = join_blocks(self.send, self.came, self.order, self.splits)
        else:
            self.send = jnp.concatenate([self.send, self.came], axis=0)


def close_round(movers, *arrays):
    came = [m.came for m in movers]
    came, arrays = lax.optimization_barrier((came, arrays))
    for m, block in zip(movers, came):
        m.came = block
    for m in movers:
        m.absorb()
    going = [m for m in movers if m.step < len(m.order)]
    sends, arrays = lax.optimization_barrier(([m.send for m in going], arrays))
    for m, block in zip(going, sends):
        m.send = block
    return arrays


def sides_of(order):
    at = my_index()
    return [lax.rem(lax.shift_right_logical(at, b), 2) for b in order]


def panels_of(other, width):
    return other.shape[1] // width


def rows_in_order(rows, first, own, size, order):
    total = len(order)
    part = rows[:, first : first + own * size]
    split = part.reshape((part.shape[0],) + (2,) * total + (own,))
    axes = [1 + (total - 1 - b) for b in order] + [1 + total, 0]
    return split.transpose(axes).reshape(size * own, part.shape[0])


def pack_plain(items, width, order):
    size = 1 << len(order)
    parts = []
    for rows, first, span, other in items:
        own = span // size
        block = mm(rows_in_order(rows, first, own, size, order), other).astype(BFLOAT)
        block = block.reshape(size, own, panels_of(other, width), width).transpose(0, 2, 1, 3)
        parts.append(block.reshape(size, -1, width))
    return jnp.concatenate(parts, axis=1)


def pack_kernel(items, width, order, natural):
    total = len(order)
    size = 1 << total
    groups = size // 4
    core_side = sides_of(order[:1])[0]
    owns = [span // size for rows, first, span, other in items]
    panels = [panels_of(other, width) for rows, first, span, other in items]
    count = len(items)
    total_rows = sum(o * p for o, p in zip(owns, panels))
    lefts, left_specs = [], []
    for (rows, first, span, other), own in zip(items, owns):
        length = rows.shape[0]
        at = first // (4 * own)
        if (4 * own) % 128 == 0:
            lefts.append(rows)
            left_specs.append(pl.BlockSpec((length, 4 * own), lambda g, core, at=at: (0, at + g)))
        else:
            lefts.append(rows.reshape(length, -1, 4 * own).transpose(1, 0, 2))
            left_specs.append(pl.BlockSpec((None, length, 4 * own), lambda g, core, at=at: (at + g, 0, 0)))
    rights, used = [], []
    for item in items:
        match = [i for i, other in enumerate(rights) if other is item[3]]
        if not match:
            rights.append(item[3])
        used.append(match[0] if match else len(rights) - 1)
    right_specs = [pl.BlockSpec(other.shape, lambda g, core: (0, 0)) for other in rights]
    rest = order[1:]

    def out_index(g, core):
        return tuple(0 if b == 0 else lax.rem(lax.shift_right_logical(g, b - 2), 2) for b in rest) + (0, 0)

    out_shape = (2,) * len(rest) + (total_rows, width)
    out_block = tuple(2 if b == 0 else None for b in rest) + (total_rows, width)
    outs = 1 if natural else 2
    if natural:
        out_shape = (size, total_rows, width)
        out_block = (4, total_rows, width)
        out_index = lambda g, core: (g, 0, 0)

    def body(core_ref, *refs):
        left_refs = refs[:count]
        right_refs = refs[count : count + len(rights)]
        pack_refs = refs[count + len(rights) : count + len(rights) + outs]
        held = refs[count + len(rights) + outs :]
        core = core_ref[0]
        for left, right, keepers in zip(left_refs, used, held):
            keepers[...] = t_mm(left[...], right_refs[right][...])
        if natural:
            targets = [(pack_refs[0], i, i) for i in range(4)]
        else:
            targets = [(pack_refs[0], i, 2 * (1 - core) + i) for i in range(2)]
            targets += [(pack_refs[1], i, 2 * core + i) for i in range(2)]
        for ref, near, which in targets:
            pieces = []
            for keepers, own, many in zip(held, owns, panels):
                start = which * own if natural else pl.multiple_of(which * own, 8)
                for p in range(many):
                    pieces.append(keepers[pl.ds(start, own), p * width : (p + 1) * width])
            ref[near] = jnp.concatenate(pieces, axis=0).astype(BFLOAT)

    flops = sum(2 * rows.shape[0] * span * other.shape[1] for rows, first, span, other in items)
    packed = pl.pallas_call(
        body,
        grid_spec=pltpu.PrefetchScalarGridSpec(
            num_scalar_prefetch=1,
            grid=(groups,),
            in_specs=left_specs + right_specs,
            out_specs=[pl.BlockSpec(out_block, out_index)] * outs,
            scratch_shapes=[
                pltpu.VMEM((4 * own, other.shape[1]), FLOAT)
                for own, (rows, first, span, other) in zip(owns, items)
            ],
        ),
        out_shape=[jax.ShapeDtypeStruct(out_shape, BFLOAT)] * outs,
        compiler_params=pltpu.CompilerParams(vmem_limit_bytes=32 * 1024 * 1024),
        cost_estimate=FREE,
    )(core_side.astype(jnp.int32).reshape(1), *lefts, *rights)
    if natural:
        return packed[0]
    flat = (size // 2, total_rows, width)
    return packed[0].reshape(flat), packed[1].reshape(flat)


def aligned_items(items, size):
    return all(span % (8 * size) == 0 for rows, first, span, other in items)


def pack_natural(items, width):
    bits = sum(device_bits())
    if aligned_items(items, 1 << bits):
        return pack_kernel(items, width, list(range(bits)), True)
    return pack_plain(items, width, list(range(bits))[::-1])


def pack(items, width, order):
    size = 1 << len(order)
    if aligned_items(items, size) and order[0] == 1:
        return pack_kernel(items, width, order, False)
    block = pack_plain(items, width, order)
    block = block.reshape((2, size // 2) + block.shape[1:])
    at = sides_of(order[:1])[0]
    return take(block, 1 - at), take(block, at)


class Whole:
    def __init__(self, items, width):
        self.block = pack_natural(items, width)

    def launch(self):
        flat = self.block.reshape(-1, self.block.shape[-1])
        self.sum = lax.psum_scatter(flat, ALL, scatter_dimension=0, tiled=True)

    def finish(self):
        return self.sum.astype(FLOAT)


class Chunk:
    def __init__(self, items, width, order):
        self.order = order
        self.sides = sides_of(order)
        self.send, self.keep = pack(items, width, order)
        self.step = 0

    def start(self):
        self.came = swap(self.send, self.order[self.step])
        self.step += 1

    def absorb(self):
        if self.step == len(self.order):
            self.full = (self.came.astype(FLOAT) + self.keep.astype(FLOAT))[0]
            return
        half = self.came.shape[0] // 2
        came = self.came.reshape((2, half) + self.came.shape[1:])
        keep = self.keep.reshape((2, half) + self.keep.shape[1:])
        at = self.sides[self.step]
        self.send = add_low(take(came, 1 - at), take(keep, 1 - at))
        self.keep = add_low(take(came, at), take(keep, at))


class Small(Chunk):
    def __init__(self, block, order):
        total = len(order)
        tail = block.shape[1:]
        held = block.reshape((2,) * total + tail)
        held = held.transpose([total - 1 - b for b in order] + [total + i for i in range(len(tail))])
        held = held.reshape((2, -1) + tail)
        self.order = order
        self.sides = sides_of(order)
        self.send, self.keep = take(held, 1 - self.sides[0]), take(held, self.sides[0])
        self.step = 0


def mm(left, right):
    return jnp.dot(left, right, preferred_element_type=FLOAT)


def mm_t(left, right):
    return lax.dot_general(left, right, (((1,), (1,)), ((), ())), preferred_element_type=FLOAT)


def t_mm(left, right):
    return lax.dot_general(left, right, (((0,), (0,)), ((), ())), preferred_element_type=FLOAT)


def layer_norm(stream, gain_vec):
    center = stream - jnp.mean(stream, axis=-1, keepdims=True)
    spread = jnp.mean(center * center, axis=-1, keepdims=True)
    return center * lax.rsqrt(spread + EPSILON) * gain_vec


def norm_back(stream, gain_vec, upstream):
    center = stream - jnp.mean(stream, axis=-1, keepdims=True)
    scale = lax.rsqrt(jnp.mean(center * center, axis=-1, keepdims=True) + EPSILON)
    unit = center * scale
    weighted = upstream * gain_vec
    inner = jnp.mean(weighted * unit, axis=-1, keepdims=True)
    grad = (weighted - jnp.mean(weighted, axis=-1, keepdims=True) - unit * inner) * scale
    return grad, jnp.sum(upstream * unit, axis=0)


def gelu_back(upper, upstream):
    unused, pullback = jax.vjp(jax.nn.gelu, upper)
    return pullback(upstream)[0]


def head_blocks(width, heads):
    size = width // heads
    block = max(size, 128)
    return [(h * size // block * block, block, h * size % block, size) for h in range(heads)]


def only_head(value, start, size):
    if size == value.shape[1]:
        return value
    lane = lax.broadcasted_iota(jnp.int32, value.shape, 1)
    return jnp.where((lane >= start) & (lane < start + size), value, jnp.zeros_like(value))


def head_probs(query, key, size, valid):
    scores = mm_t(query, key) * (size ** (-0.5))
    if valid is not None:
        lane = lax.broadcasted_iota(jnp.int32, scores.shape, 1)
        scores = jnp.where(lane < valid, scores, NEGATIVE)
    expo = jnp.exp(scores - jnp.max(scores, axis=-1, keepdims=True))
    return expo / jnp.sum(expo, axis=-1, keepdims=True)


def attend_block(q_ref, k_ref, v_ref, q_at, k_at, v_at, out_ref, heads, valid):
    width = out_ref.shape[1]
    parts = {}
    for base, block, start, size in head_blocks(width, heads):
        q = only_head(q_ref[:, q_at + base : q_at + base + block], start, size)
        k = k_ref[:, k_at + base : k_at + base + block]
        v = only_head(v_ref[:, v_at + base : v_at + base + block], start, size)
        part = mm(head_probs(q, k, size, valid).astype(BFLOAT), v)
        parts[base] = part if base not in parts else parts[base] + part
        if start + size == block:
            out_ref[:, base : base + block] = parts[base].astype(BFLOAT)


def attend_block_back(
    q_ref, k_ref, v_ref, q_at, k_at, v_at, g_ref, dq_ref, dk_ref, dv_ref, heads, valid
):
    width = g_ref.shape[1]
    parts = {}
    for base, block, start, size in head_blocks(width, heads):
        q = only_head(q_ref[:, q_at + base : q_at + base + block], start, size)
        k = only_head(k_ref[:, k_at + base : k_at + base + block], start, size)
        v = v_ref[:, v_at + base : v_at + base + block]
        g = only_head(g_ref[:, base : base + block], start, size)
        probs = head_probs(q, k, size, valid)
        grad_probs = mm_t(g, v)
        inner = jnp.sum(grad_probs * probs, axis=-1, keepdims=True)
        grad_scores = (probs * (grad_probs - inner)).astype(BFLOAT)
        scale = size ** (-0.5)
        news = (mm(grad_scores, k) * scale, t_mm(grad_scores, q) * scale, t_mm(probs.astype(BFLOAT), g))
        if base in parts:
            news = tuple(x + y for x, y in zip(parts[base], news))
        parts[base] = news
        if start + size == block:
            for ref, at, new in zip((dq_ref, dk_ref, dv_ref), (q_at, k_at, v_at), news):
                ref[:, at + base : at + base + block] = new.astype(BFLOAT)


def vmem_call(body, count, outs, scalar, flops, *operands):
    return pl.pallas_call(
        body,
        in_specs=[pl.BlockSpec(memory_space=pltpu.SMEM)] + [pl.BlockSpec(memory_space=pltpu.VMEM)] * count,
        out_specs=[pl.BlockSpec(memory_space=pltpu.VMEM)] * len(outs),
        out_shape=[jax.ShapeDtypeStruct(shape, BFLOAT) for shape in outs],
        compiler_params=pltpu.CompilerParams(vmem_limit_bytes=32 * 1024 * 1024),
        cost_estimate=FREE,
    )(scalar, *operands)


def cross_attend(text, image, length):
    width = text.shape[1] // 3

    def body(len_ref, text_ref, image_ref, t_ref, i_ref):
        attend_block(text_ref, image_ref, image_ref, 0, width, 2 * width, t_ref, H_C, None)
        attend_block(image_ref, text_ref, text_ref, 0, width, 2 * width, i_ref, H_C, len_ref[0])

    flops = 8 * text.shape[0] * image.shape[0] * width * 8
    outs = [(text.shape[0], width), (image.shape[0], width)]
    return vmem_call(body, 2, outs, length, flops, text, image)


def cross_attend_back(text, image, length, t_grad, i_grad):
    width = text.shape[1] // 3

    def body(len_ref, text_ref, image_ref, tg_ref, ig_ref, dt_ref, di_ref):
        attend_block_back(
            text_ref, image_ref, image_ref, 0, width, 2 * width, tg_ref, dt_ref, di_ref, di_ref, H_C, None
        )
        attend_block_back(
            image_ref, text_ref, text_ref, 0, width, 2 * width, ig_ref, di_ref, dt_ref, dt_ref, H_C, len_ref[0]
        )

    flops = 20 * text.shape[0] * image.shape[0] * width * 8
    return vmem_call(body, 4, [text.shape, image.shape], length, flops, text, image, t_grad, i_grad)


def self_attend(packed, heads, length, masked):
    width = packed.shape[1] // 3

    def body(len_ref, ref, out_ref):
        attend_block(ref, ref, ref, 0, width, 2 * width, out_ref, heads, len_ref[0] if masked else None)

    flops = 4 * packed.shape[0] * packed.shape[0] * width * 8
    return vmem_call(body, 1, [(packed.shape[0], width)], length, flops, packed)[0]


def self_attend_back(packed, heads, length, masked, grad):
    width = packed.shape[1] // 3

    def body(len_ref, ref, g_ref, d_ref):
        attend_block_back(
            ref, ref, ref, 0, width, 2 * width, g_ref, d_ref, d_ref, d_ref, heads, len_ref[0] if masked else None
        )

    flops = 10 * packed.shape[0] * packed.shape[0] * width * 8
    return vmem_call(body, 2, [packed.shape], length, flops, packed, grad)[0]


def tail_forward(residual, attn_low, out_mat, up_mat, down_mat, gain_pair):
    first_sum = residual + mm(attn_low, out_mat)
    first_norm = layer_norm(first_sum, gain_pair[0])
    hidden_low = first_norm.astype(BFLOAT)
    upper = mm(hidden_low, up_mat)
    active = jax.nn.gelu(upper).astype(BFLOAT)
    second_sum = first_norm + mm(active, down_mat)
    return layer_norm(second_sum, gain_pair[1]), (first_sum, hidden_low, upper, active, second_sum)


def tail_backward(grad_result, kept, attn_low, out_mat, up_mat, down_mat, gain_pair, down_natural):
    first_sum, hidden_low, upper, active, second_sum = kept
    grad_second, gain_two = norm_back(second_sum, gain_pair[1], grad_result)
    low = grad_second.astype(BFLOAT)
    grad_down = whole_item(active, low) if down_natural else whole_item(low, active)
    grad_upper = gelu_back(upper, mm_t(low, down_mat)).astype(BFLOAT)
    grad_up = whole_item(grad_upper, hidden_low)
    grad_norm = grad_second + mm_t(grad_upper, up_mat)
    grad_first, gain_one = norm_back(first_sum, gain_pair[0], grad_norm)
    grad_first_low = grad_first.astype(BFLOAT)
    grad_out = whole_item(attn_low, grad_first_low)
    grad_attn = mm_t(grad_first_low, out_mat).astype(BFLOAT)
    return grad_first, grad_attn, [grad_down, grad_up, grad_out], [gain_one, gain_two]


def project(stream_low, proj):
    return mm(stream_low, proj).astype(BFLOAT)


def whole_item(rows, other):
    return (rows, 0, rows.shape[1], other)


def third_items(packed, other):
    span = packed.shape[1] // 3
    return [(packed, e * span, span, other) for e in range(3)]


def side(shards):
    return jnp.concatenate(shards, axis=1)


def on_device(
    text_input,
    image_input,
    caption_lengths,
    text_cotangent,
    image_cotangent,
    cross_text_proj,
    cross_image_proj,
    cross_text_out,
    cross_image_out,
    cross_text_up,
    cross_text_down,
    cross_image_up,
    cross_image_down,
    self_text_proj,
    self_text_out,
    self_text_up,
    self_text_down,
    self_image_proj,
    self_image_out,
    self_image_up,
    self_image_down,
    text_gains,
    image_gains,
):
    d_t = text_input.shape[2]
    d_v = image_input.shape[2]
    co = cross_text_proj.shape[2]
    ff_t = cross_text_up.shape[1]
    n_text = text_input.shape[1]

    size = lax.axis_size("dp") * lax.axis_size("seq")
    bits = sum(device_bits())
    by_permute = size == 1 << bits and all(
        m.shape[-2] % 8 == 0 for m in (cross_text_out, cross_text_down, self_text_down)
    )

    def gather_columns(parts):
        return lax.all_gather(side(parts), ALL, axis=0, tiled=True)

    own_t, own_v = d_t // size, d_v // size
    own_f, own_c = ff_t // size, co // size
    text_parts = list(cross_text_proj) + [cross_text_up] + list(self_text_proj)
    text_wide = gather_columns(text_parts + [self_text_out, self_text_up])
    image_parts = [cross_image_out, cross_image_up, cross_image_down] + list(self_image_proj)
    image_wide = gather_columns(image_parts + [self_image_out, self_image_up, self_image_down])
    w_ctp = text_wide[:, : 3 * co]

    high = list(range(3, bits))[::-1]
    x_first = high + [2, 0, 1]
    y_first = high + [0, 2, 1]
    shards = [
        (side(list(cross_image_proj)), y_first, None),
        (jnp.concatenate([cross_text_down, cross_text_out], axis=0), x_first, [own_f, own_c]),
        (self_text_down, x_first, None),
    ]

    panel = 128
    my_len = lax.dynamic_index_in_dim(caption_lengths, lax.axis_index("seq"), 0, keepdims=True)
    x_t = text_input[0]
    x_v = image_input[0]

    if by_permute:
        movers = [Gather(*item) for item in shards]
        for turn_at in range(bits):
            active = movers[:2] + ([movers[2]] if turn_at >= 2 else [])
            for m in active:
                m.start()
            close_round(active)
        w_cip = movers[0].full[0]
        w_ctd, w_cto = movers[1].full
        movers[2].start()
        t_packed = project(x_t, w_ctp)
        i_packed = project(x_v, w_cip)
        t_attn, i_attn = cross_attend(t_packed, i_packed, my_len)
        t_attn, i_attn = close_round(movers[2:], t_attn, i_attn)
        movers[2].start()
    else:
        full = [lax.all_gather(shard, ALL, axis=0) for shard, order, splits in shards]
        w_ctd, w_cto = full[1][:, :own_f], full[1][:, own_f:]
        w_cip, w_ctd, w_cto, w_std = (w.reshape(-1, w.shape[-1]) for w in (full[0], w_ctd, w_cto, full[2]))
        t_packed = project(x_t, w_ctp)
        i_packed = project(x_v, w_cip)
        t_attn, i_attn = cross_attend(t_packed, i_packed, my_len)

    w_ctu = text_wide[:, 3 * co : 3 * co + ff_t]
    text_self = text_wide[:, 3 * co + ff_t :]
    w_stp, w_sto, w_stu = text_self[:, : 3 * d_t], text_self[:, 3 * d_t : 4 * d_t], text_self[:, 4 * d_t :]

    def halving(*picks):
        return [1] + list(picks) + [b for b in range(bits) if b != 1 and b not in picks]

    t_cross, t_kept = tail_forward(x_t.astype(FLOAT), t_attn, w_cto, w_ctu, w_ctd, text_gains[0:2])
    t_low = t_cross.astype(BFLOAT)
    if by_permute:
        t_cross, t_kept = close_round(movers[2:], t_cross, t_kept)
        w_std = movers[2].full[0]
        t_low = t_cross.astype(BFLOAT)
    st_packed = project(t_low, w_stp)
    st_attn = self_attend(st_packed, H_T, my_len, True)
    t_final, st_kept = tail_forward(t_cross, st_attn, w_sto, w_stu, w_std, text_gains[2:4])
    t_res, t_ga, t_pairs, t_gain_s = tail_backward(
        text_cotangent[0].astype(FLOAT), st_kept, st_attn, w_sto, w_stu, w_std, text_gains[2:4], False
    )
    def start(*movers):
        for m in movers:
            if m.step < bits:
                m.start()

    def by_owner(packed, own):
        rows = packed.shape[0]
        blocks = packed.reshape(rows, 3, size, own).transpose(2, 0, 1, 3).reshape(size, rows, 3 * own)
        return jnp.pad(blocks, ((0, 0), (0, -rows % 8), (0, 3 * (own_v - own))))

    if by_permute:
        tall = -(-x_t.shape[0] // 8) * 8
        seen = [jnp.pad(m, ((0, tall - m.shape[0]), (0, 0))) for m in (x_t, t_low)]
        seen = jnp.concatenate([x_v.reshape(-1, d_t)] + seen, axis=0)
        seen = lax.all_gather(seen, ALL, axis=0)
    c1a = Chunk(t_pairs[:1], d_t, halving(2, 0))
    c1b = Chunk(t_pairs[1:], d_t, halving(0, 2))
    t_ga, t_res, i_attn = close_round([], t_ga, t_res, i_attn)

    start(c1a, c1b)
    st_grads = self_attend_back(st_packed, H_T, my_len, True, t_ga)
    t_back = t_res + mm_t(st_grads, w_stp)
    st_grads, t_back, i_attn = close_round([c1a, c1b], st_grads, t_back, i_attn)

    start(c1a, c1b)
    t_res, t_ga, t_pairs, t_gain_c = tail_backward(
        t_back, t_kept, t_attn, w_cto, w_ctu, w_ctd, text_gains[0:2], True
    )
    c3a = Chunk([t_pairs[0], t_pairs[2]], d_t, halving(2, 0))
    c3b = Chunk(t_pairs[1:2], d_t, halving(0, 2))
    c3a.send, c3a.keep, c3b.send, c3b.keep, t_res, t_ga, i_attn = close_round(
        [c1a, c1b], c3a.send, c3a.keep, c3b.send, c3b.keep, t_res, t_ga, i_attn
    )
    start(c1a, c1b, c3a, c3b)
    (i_attn,) = close_round([c1a, c1b, c3a, c3b], i_attn)

    w_cio, w_ciu, w_cid = (image_wide[:, i * d_v : (i + 1) * d_v] for i in range(3))
    w_sip = image_wide[:, 3 * d_v : 6 * d_v]
    w_sio, w_siu, w_sid = (image_wide[:, (6 + i) * d_v : (7 + i) * d_v] for i in range(3))

    start(c3a, c3b, c1a, c1b)
    i_cross, i_kept = tail_forward(x_v.astype(FLOAT), i_attn, w_cio, w_ciu, w_cid, image_gains[0:2])
    i_low = i_cross.astype(BFLOAT)
    si_packed = project(i_low, w_sip)
    si_attn = self_attend(si_packed, H_V, my_len, False)
    i_final, si_kept = tail_forward(i_cross, si_attn, w_sio, w_siu, w_sid, image_gains[2:4])
    i_res, i_ga, i_pairs, i_gain_s = tail_backward(
        image_cotangent[0].astype(FLOAT), si_kept, si_attn, w_sio, w_siu, w_sid, image_gains[2:4], False
    )
    c1i = Chunk(i_pairs, d_v, halving(0, 2))
    c1i.send, c1i.keep, i_ga, i_res = close_round(
        [c1a, c1b, c3a, c3b], c1i.send, c1i.keep, i_ga, i_res
    )
    if by_permute:
        seen_low_v = lax.all_gather(i_low.reshape(-1, d_t), ALL, axis=0)

    start(c1i, c3a, c3b)
    si_grads = self_attend_back(si_packed, H_V, my_len, False, i_ga)
    i_back = i_res + mm_t(si_grads, w_sip)
    self_blocks = (st_grads, si_grads)
    if by_permute:
        self_blocks = (by_owner(st_grads, own_t), by_owner(si_grads, own_v))
    self_blocks, i_back = close_round([c1i, c3a, c3b], self_blocks, i_back)

    start(c1i, c3a, c3b)
    i_res, i_ga, i_pairs, i_gain_c = tail_backward(
        i_back, i_kept, i_attn, w_cio, w_ciu, w_cid, image_gains[0:2], True
    )
    c3x = Chunk(i_pairs[:1], d_v, halving(2, 0))
    c3y = Chunk(i_pairs[1:], d_v, halving(0, 2))
    c3x.send, c3x.keep, c3y.send, c3y.keep, i_res, i_ga, t_ga = close_round(
        [c1i, c3a, c3b], c3x.send, c3x.keep, c3y.send, c3y.keep, i_res, i_ga, t_ga
    )

    start(c3x, c3y, c1i)
    t_grads, i_grads = cross_attend_back(t_packed, i_packed, my_len, t_ga, i_ga)
    t_grads, i_grads = close_round([c3x, c3y, c1i], t_grads, i_grads)

    t_gain = jnp.stack(t_gain_c + t_gain_s)
    i_gain = jnp.stack(i_gain_c + i_gain_s)
    start(c3x, c3y, c1i)
    blocks = t_grads
    if by_permute:
        gain_rows = [t_gain.reshape(4, size, own_t), i_gain.reshape(4, size, own_v)]
        gain_rows = [
            jnp.pad(g.astype(BFLOAT), ((0, 0), (0, 0), (0, 3 * own_v - g.shape[2]))) for g in gain_rows
        ]
        gain_rows = jnp.concatenate(gain_rows, axis=0).transpose(1, 0, 2)
        blocks = [by_owner(t_grads, own_c), by_owner(i_grads, own_c), gain_rows, *self_blocks]
        blocks = jnp.concatenate(blocks, axis=1)
    (blocks,) = close_round([c3x, c3y, c1i], blocks)
    start(c3x, c3y, c3a, c3b)
    text_input_grad = t_res + mm_t(t_grads, w_ctp)
    image_input_grad = i_res + mm_t(i_grads, w_cip)
    slices, rows_all = t_low, t_low
    if by_permute:
        slices = lax.all_to_all(blocks, ALL, split_axis=0, concat_axis=0, tiled=True)
        short = x_v.size // d_t
        rows_all = (
            seen_low_v.reshape(-1, d_v),
            seen[:, :short].reshape(-1, d_v),
            seen[:, short : short + tall].reshape(-1, d_t),
            seen[:, short + tall :].reshape(-1, d_t),
        )
    text_input_grad, image_input_grad, rows_all = close_round(
        [c3x, c3y, c3a, c3b], text_input_grad, image_input_grad, rows_all
    )
    start(c3x, c3y, c1a, c1b, c1i)

    def slices_grad(rows, part, own):
        grad = t_mm(rows, part.reshape(-1, part.shape[2]))[:, : 3 * own]
        return grad.reshape(grad.shape[0], 3, own).transpose(1, 0, 2)

    self_grads, cross_grads = t_low, t_low
    if by_permute:
        all_low_v, all_v, all_t, all_low_t = rows_all
        wide_v = x_v.shape[0]
        tall_v = -(-wide_v // 8) * 8
        selves = tall + tall_v + 8
        gain_sum = jnp.sum(slices[:, tall + tall_v : selves].astype(FLOAT), axis=0)
        self_grads = (
            slices_grad(all_low_t, slices[:, selves : selves + tall], own_t),
            slices_grad(all_low_v, slices[:, selves + tall : selves + tall + wide_v], own_v),
            gain_sum,
        )
    (self_grads,) = close_round([c3x, c3y, c1a, c1b, c1i], self_grads)
    start(c3x, c3y)
    if by_permute:
        cross_grads = (
            slices_grad(all_t, slices[:, :tall], own_c),
            slices_grad(all_v, slices[:, tall : tall + wide_v], own_c),
        )
    (cross_grads,) = close_round([c3x, c3y], cross_grads)
    for m in (c1a, c1b, c3a, c3b, c1i, c3x, c3y):
        while m.step < bits:
            m.start()
            m.absorb()

    if by_permute:
        o_stp, o_sip, gain_sum = self_grads
        o_ctp, o_cip = cross_grads
        o_tg, o_ig = gain_sum[:4, :own_t], gain_sum[4:, :own_v]
    else:

        def by_scatter(packed, rows):
            whole = Whole(third_items(packed, rows), rows.shape[1])
            whole.launch()
            block = whole.finish()
            return block.reshape(3, block.shape[0] // 3, block.shape[1]).transpose(0, 2, 1)

        o_stp, o_sip = by_scatter(self_blocks[0], t_low), by_scatter(self_blocks[1], i_low)
        o_ctp, o_cip = by_scatter(t_grads, x_t), by_scatter(i_grads, x_v)
        at = my_index()
        t_gain, i_gain = lax.psum(t_gain, ALL), lax.psum(i_gain, ALL)
        o_tg = lax.dynamic_slice_in_dim(t_gain, at * own_t, own_t, 1)
        o_ig = lax.dynamic_slice_in_dim(i_gain, at * own_v, own_v, 1)

    def cut(block, rows):
        out, at = [], 0
        for r in rows:
            out.append(block[at : at + r])
            at += r
        return out

    (g_std,) = cut(c1a.full, (ff_t // d_t * own_t,))
    g_stu, g_sto = cut(c1b.full, (own_f, own_t))
    g_sid, g_siu, g_sio = cut(c1i.full, (own_v,) * 3)
    g_ctd, g_cto = cut(c3a.full, (own_f, own_c))
    g_ctu, g_cid = c3b.full, c3x.full
    g_ciu, g_cio = cut(c3y.full, (own_v,) * 2)
    g_std = g_std.reshape(ff_t // d_t, own_t, d_t).transpose(1, 0, 2).reshape(own_t, ff_t)

    o_stu, o_ctu, o_ctd = g_stu.T, g_ctu.T, g_ctd
    o_std, o_sto = g_std.T, g_sto
    o_sid, o_siu, o_sio = g_sid.T, g_siu.T, g_sio
    o_cid, o_ciu, o_cio, o_cto = g_cid, g_ciu.T, g_cio, g_cto
    return (
        t_final.astype(BFLOAT)[None],
        i_final.astype(BFLOAT)[None],
        text_input_grad[None],
        image_input_grad[None],
        o_ctp,
        o_cip,
        o_cto,
        o_cio,
        o_ctu,
        o_ctd,
        o_ciu,
        o_cid,
        o_stp,
        o_sto,
        o_stu,
        o_std,
        o_sip,
        o_sio,
        o_siu,
        o_sid,
        o_tg,
        o_ig,
    )


def solution(mesh):
    row = P(ALL, None)
    batch = P(ALL, None, None)
    col = P(None, ALL)
    proj = P(None, ALL, None)
    proj_grad = P(None, None, ALL)
    in_specs = (batch, batch, P("dp"), batch, batch, proj, proj, row, row, row, row, row, row)
    in_specs += (proj, row, row, row, proj, row, row, row, P(), P())
    out_specs = (batch, batch, batch, batch, proj_grad, proj_grad, row, row, col, row, col, row)
    out_specs += (proj_grad, row, col, col, proj_grad, row, col, col, col, col)
    return jax.shard_map(
        on_device, mesh=mesh, in_specs=in_specs, out_specs=out_specs, check_vma=False
    )
```

```python
import jax
import jax.numpy as jnp
from jax import lax
from jax.experimental import pallas as pl
from jax.experimental.pallas import tpu as pltpu
from jax.sharding import PartitionSpec as P

H_T = 12
H_V = 8
H_C = 8

EPSILON = 1e-05
NEGATIVE = -1000000000.0
FLOAT = jnp.float32
BFLOAT = jnp.bfloat16
ALL = ("dp", "seq")
FREE = pl.CostEstimate(flops=0, bytes_accessed=0, transcendentals=0)


def device_bits():
    return (lax.axis_size("dp").bit_length() - 1, lax.axis_size("seq").bit_length() - 1)


def my_index():
    return lax.axis_index("dp") * lax.axis_size("seq") + lax.axis_index("seq")


def swap(block, bit):
    size = lax.axis_size("dp") * lax.axis_size("seq")
    return lax.ppermute(block, ALL, [(i, i ^ (1 << bit)) for i in range(size)])


def orders():
    dp_bits, seq_bits = device_bits()
    total = dp_bits + seq_bits
    core = seq_bits
    rest = [b for b in range(total) if b != core]
    seq_first = [core] + rest
    dp_first = [core] + rest[1:2] + rest[0:1] + rest[2:]
    far_first = [core] + rest[2:3] + rest[1:2] + rest[0:1] + rest[3:]
    return seq_first, dp_first, far_first


def take(block, which):
    return lax.dynamic_index_in_dim(block, which, 0, keepdims=False)


def add_low(left, right):
    return (left.astype(FLOAT) + right.astype(FLOAT)).astype(BFLOAT)


def join_blocks(held, came, order, splits):
    count, rows, width = held.shape
    bits = len(order)
    near = order.index(0)
    low = 1 << near
    pairs = (count // (2 * low), 2, low, rows, width)

    def out_index(j, at):
        place = jnp.int32(0)
        for k, b in enumerate(order[:-1]):
            if b != 0:
                bit = lax.rem(lax.shift_right_logical(j, k if k < near else k - 1), 2)
                place = place + lax.shift_left(bit, b)
        block = jnp.bitwise_xor(at[0], place)
        return (lax.shift_right_logical(block, 2), 0, 0, 0, 0)

    def body(at_ref, held_ref, came_ref, *outs):
        side = lax.rem(lax.shift_right_logical(at_ref[0], 1), 2)
        mine = lax.rem(at_ref[0], 2)
        start = 0
        for out, many in zip(outs, splits):
            for step in range(2):
                y = jnp.bitwise_xor(mine, step)
                out[0, side, y] = held_ref[0, step, 0, start : start + many]
                out[0, 1 - side, y] = came_ref[0, step, 0, start : start + many]
            start += many

    def in_index(j, at):
        return (lax.div(j, low), 0, lax.rem(j, low), 0, 0)

    outs = pl.pallas_call(
        body,
        grid_spec=pltpu.PrefetchScalarGridSpec(
            num_scalar_prefetch=1,
            grid=(count // 2,),
            in_specs=[pl.BlockSpec((1, 2, 1, rows, width), in_index)] * 2,
            out_specs=[pl.BlockSpec((1, 2, 2, many, width), out_index) for many in splits],
        ),
        out_shape=[
            jax.ShapeDtypeStruct((1 << (bits - 2), 2, 2, many, width), held.dtype) for many in splits
        ],
        compiler_params=pltpu.CompilerParams(vmem_limit_bytes=32 * 1024 * 1024),
        cost_estimate=FREE,
    )(my_index().astype(jnp.int32).reshape(1), held.reshape(pairs), came.reshape(pairs))
    return [out.reshape(-1, width) for out in outs]


class Gather:
    def __init__(self, shard, order, splits=None):
        self.order = order
        self.send = shard[None]
        self.splits = splits or [shard.shape[0]]
        self.step = 0

    def start(self):
        self.came = swap(self.send, self.order[self.step])
        self.step += 1

    def absorb(self):
        if self.step == len(self.order):
            self.full = join_blocks(self.send, self.came, self.order, self.splits)
        else:
            self.send = jnp.concatenate([self.send, self.came], axis=0)


def close_round(movers, *arrays):
    came = [m.came for m in movers]
    came, arrays = lax.optimization_barrier((came, arrays))
    for m, block in zip(movers, came):
        m.came = block
    for m in movers:
        m.absorb()
    going = [m for m in movers if m.step < len(m.order)]
    sends, arrays = lax.optimization_barrier(([m.send for m in going], arrays))
    for m, block in zip(going, sends):
        m.send = block
    return arrays


def sides_of(order):
    at = my_index()
    return [lax.rem(lax.shift_right_logical(at, b), 2) for b in order]


def panels_of(other, width):
    return other.shape[1] // width


def rows_in_order(rows, first, own, size, order):
    total = len(order)
    part = rows[:, first : first + own * size]
    split = part.reshape((part.shape[0],) + (2,) * total + (own,))
    axes = [1 + (total - 1 - b) for b in order] + [1 + total, 0]
    return split.transpose(axes).reshape(size * own, part.shape[0])


def pack_plain(items, width, order):
    size = 1 << len(order)
    parts = []
    for rows, first, span, other in items:
        own = span // size
        block = mm(rows_in_order(rows, first, own, size, order), other).astype(BFLOAT)
        block = block.reshape(size, own, panels_of(other, width), width).transpose(0, 2, 1, 3)
        parts.append(block.reshape(size, -1, width))
    return jnp.concatenate(parts, axis=1)


def pack_kernel(items, width, order, natural):
    total = len(order)
    size = 1 << total
    groups = size // 4
    core_side = sides_of(order[:1])[0]
    owns = [span // size for rows, first, span, other in items]
    panels = [panels_of(other, width) for rows, first, span, other in items]
    count = len(items)
    total_rows = sum(o * p for o, p in zip(owns, panels))
    lefts, left_specs = [], []
    for (rows, first, span, other), own in zip(items, owns):
        length = rows.shape[0]
        at = first // (4 * own)
        if (4 * own) % 128 == 0:
            lefts.append(rows)
            left_specs.append(pl.BlockSpec((length, 4 * own), lambda g, core, at=at: (0, at + g)))
        else:
            lefts.append(rows.reshape(length, -1, 4 * own).transpose(1, 0, 2))
            left_specs.append(pl.BlockSpec((None, length, 4 * own), lambda g, core, at=at: (at + g, 0, 0)))
    rights, used = [], []
    for item in items:
        match = [i for i, other in enumerate(rights) if other is item[3]]
        if not match:
            rights.append(item[3])
        used.append(match[0] if match else len(rights) - 1)
    right_specs = [pl.BlockSpec(other.shape, lambda g, core: (0, 0)) for other in rights]
    rest = order[1:]

    def out_index(g, core):
        return tuple(0 if b == 0 else lax.rem(lax.shift_right_logical(g, b - 2), 2) for b in rest) + (0, 0)

    out_shape = (2,) * len(rest) + (total_rows, width)
    out_block = tuple(2 if b == 0 else None for b in rest) + (total_rows, width)
    outs = 1 if natural else 2
    if natural:
        out_shape = (size, total_rows, width)
        out_block = (4, total_rows, width)
        out_index = lambda g, core: (g, 0, 0)

    def body(core_ref, *refs):
        left_refs = refs[:count]
        right_refs = refs[count : count + len(rights)]
        pack_refs = refs[count + len(rights) : count + len(rights) + outs]
        held = refs[count + len(rights) + outs :]
        core = core_ref[0]
        for left, right, keepers in zip(left_refs, used, held):
            keepers[...] = t_mm(left[...], right_refs[right][...])
        if natural:
            targets = [(pack_refs[0], i, i) for i in range(4)]
        else:
            targets = [(pack_refs[0], i, 2 * (1 - core) + i) for i in range(2)]
            targets += [(pack_refs[1], i, 2 * core + i) for i in range(2)]
        for ref, near, which in targets:
            pieces = []
            for keepers, own, many in zip(held, owns, panels):
                start = which * own if natural else pl.multiple_of(which * own, 8)
                for p in range(many):
                    pieces.append(keepers[pl.ds(start, own), p * width : (p + 1) * width])
            ref[near] = jnp.concatenate(pieces, axis=0).astype(BFLOAT)

    flops = sum(2 * rows.shape[0] * span * other.shape[1] for rows, first, span, other in items)
    packed = pl.pallas_call(
        body,
        grid_spec=pltpu.PrefetchScalarGridSpec(
            num_scalar_prefetch=1,
            grid=(groups,),
            in_specs=left_specs + right_specs,
            out_specs=[pl.BlockSpec(out_block, out_index)] * outs,
            scratch_shapes=[
                pltpu.VMEM((4 * own, other.shape[1]), FLOAT)
                for own, (rows, first, span, other) in zip(owns, items)
            ],
        ),
        out_shape=[jax.ShapeDtypeStruct(out_shape, BFLOAT)] * outs,
        compiler_params=pltpu.CompilerParams(vmem_limit_bytes=32 * 1024 * 1024),
        cost_estimate=FREE,
    )(core_side.astype(jnp.int32).reshape(1), *lefts, *rights)
    if natural:
        return packed[0]
    flat = (size // 2, total_rows, width)
    return packed[0].reshape(flat), packed[1].reshape(flat)


def aligned_items(items, size):
    return all(span % (8 * size) == 0 for rows, first, span, other in items)


def pack_natural(items, width):
    bits = sum(device_bits())
    if aligned_items(items, 1 << bits):
        return pack_kernel(items, width, list(range(bits)), True)
    return pack_plain(items, width, list(range(bits))[::-1])


def pack(items, width, order):
    size = 1 << len(order)
    if aligned_items(items, size) and order[0] == 1:
        return pack_kernel(items, width, order, False)
    block = pack_plain(items, width, order)
    block = block.reshape((2, size // 2) + block.shape[1:])
    at = sides_of(order[:1])[0]
    return take(block, 1 - at), take(block, at)


class Whole:
    def __init__(self, items, width):
        self.block = pack_natural(items, width)

    def launch(self):
        flat = self.block.reshape(-1, self.block.shape[-1])
        self.sum = lax.psum_scatter(flat, ALL, scatter_dimension=0, tiled=True)

    def finish(self):
        return self.sum.astype(FLOAT)


class Chunk:
    def __init__(self, items, width, order):
        self.order = order
        self.sides = sides_of(order)
        self.send, self.keep = pack(items, width, order)
        self.step = 0

    def start(self):
        self.came = swap(self.send, self.order[self.step])
        self.step += 1

    def absorb(self):
        if self.step == len(self.order):
            self.full = (self.came.astype(FLOAT) + self.keep.astype(FLOAT))[0]
            return
        half = self.came.shape[0] // 2
        came = self.came.reshape((2, half) + self.came.shape[1:])
        keep = self.keep.reshape((2, half) + self.keep.shape[1:])
        at = self.sides[self.step]
        self.send = add_low(take(came, 1 - at), take(keep, 1 - at))
        self.keep = add_low(take(came, at), take(keep, at))


class Small(Chunk):
    def __init__(self, block, order):
        total = len(order)
        tail = block.shape[1:]
        held = block.reshape((2,) * total + tail)
        held = held.transpose([total - 1 - b for b in order] + [total + i for i in range(len(tail))])
        held = held.reshape((2, -1) + tail)
        self.order = order
        self.sides = sides_of(order)
        self.send, self.keep = take(held, 1 - self.sides[0]), take(held, self.sides[0])
        self.step = 0


def mm(left, right):
    return jnp.dot(left, right, preferred_element_type=FLOAT)


def mm_t(left, right):
    return lax.dot_general(left, right, (((1,), (1,)), ((), ())), preferred_element_type=FLOAT)


def t_mm(left, right):
    return lax.dot_general(left, right, (((0,), (0,)), ((), ())), preferred_element_type=FLOAT)


def layer_norm(stream, gain_vec):
    center = stream - jnp.mean(stream, axis=-1, keepdims=True)
    spread = jnp.mean(center * center, axis=-1, keepdims=True)
    return center * lax.rsqrt(spread + EPSILON) * gain_vec


def norm_back(stream, gain_vec, upstream):
    center = stream - jnp.mean(stream, axis=-1, keepdims=True)
    scale = lax.rsqrt(jnp.mean(center * center, axis=-1, keepdims=True) + EPSILON)
    unit = center * scale
    weighted = upstream * gain_vec
    inner = jnp.mean(weighted * unit, axis=-1, keepdims=True)
    grad = (weighted - jnp.mean(weighted, axis=-1, keepdims=True) - unit * inner) * scale
    return grad, jnp.sum(upstream * unit, axis=0)


def gelu_back(upper, upstream):
    unused, pullback = jax.vjp(jax.nn.gelu, upper)
    return pullback(upstream)[0]


def head_blocks(width, heads):
    size = width // heads
    block = max(size, 128)
    return [(h * size // block * block, block, h * size % block, size) for h in range(heads)]


def only_head(value, start, size):
    if size == value.shape[1]:
        return value
    lane = lax.broadcasted_iota(jnp.int32, value.shape, 1)
    return jnp.where((lane >= start) & (lane < start + size), value, jnp.zeros_like(value))


def head_probs(query, key, size, valid):
    scores = mm_t(query, key) * (size ** (-0.5))
    if valid is not None:
        lane = lax.broadcasted_iota(jnp.int32, scores.shape, 1)
        scores = jnp.where(lane < valid, scores, NEGATIVE)
    expo = jnp.exp(scores - jnp.max(scores, axis=-1, keepdims=True))
    return expo / jnp.sum(expo, axis=-1, keepdims=True)


def attend_block(q_ref, k_ref, v_ref, q_at, k_at, v_at, out_ref, heads, valid):
    width = out_ref.shape[1]
    parts = {}
    for base, block, start, size in head_blocks(width, heads):
        q = only_head(q_ref[:, q_at + base : q_at + base + block], start, size)
        k = k_ref[:, k_at + base : k_at + base + block]
        v = only_head(v_ref[:, v_at + base : v_at + base + block], start, size)
        part = mm(head_probs(q, k, size, valid).astype(BFLOAT), v)
        parts[base] = part if base not in parts else parts[base] + part
        if start + size == block:
            out_ref[:, base : base + block] = parts[base].astype(BFLOAT)


def attend_block_back(
    q_ref, k_ref, v_ref, q_at, k_at, v_at, g_ref, dq_ref, dk_ref, dv_ref, heads, valid
):
    width = g_ref.shape[1]
    parts = {}
    for base, block, start, size in head_blocks(width, heads):
        q = only_head(q_ref[:, q_at + base : q_at + base + block], start, size)
        k = only_head(k_ref[:, k_at + base : k_at + base + block], start, size)
        v = v_ref[:, v_at + base : v_at + base + block]
        g = only_head(g_ref[:, base : base + block], start, size)
        probs = head_probs(q, k, size, valid)
        grad_probs = mm_t(g, v)
        inner = jnp.sum(grad_probs * probs, axis=-1, keepdims=True)
        grad_scores = (probs * (grad_probs - inner)).astype(BFLOAT)
        scale = size ** (-0.5)
        news = (mm(grad_scores, k) * scale, t_mm(grad_scores, q) * scale, t_mm(probs.astype(BFLOAT), g))
        if base in parts:
            news = tuple(x + y for x, y in zip(parts[base], news))
        parts[base] = news
        if start + size == block:
            for ref, at, new in zip((dq_ref, dk_ref, dv_ref), (q_at, k_at, v_at), news):
                ref[:, at + base : at + base + block] = new.astype(BFLOAT)


def vmem_call(body, count, outs, scalar, flops, *operands):
    return pl.pallas_call(
        body,
        in_specs=[pl.BlockSpec(memory_space=pltpu.SMEM)] + [pl.BlockSpec(memory_space=pltpu.VMEM)] * count,
        out_specs=[pl.BlockSpec(memory_space=pltpu.VMEM)] * len(outs),
        out_shape=[jax.ShapeDtypeStruct(shape, BFLOAT) for shape in outs],
        compiler_params=pltpu.CompilerParams(vmem_limit_bytes=32 * 1024 * 1024),
        cost_estimate=FREE,
    )(scalar, *operands)


def cross_attend(text, image, length):
    width = text.shape[1] // 3

    def body(len_ref, text_ref, image_ref, t_ref, i_ref):
        attend_block(text_ref, image_ref, image_ref, 0, width, 2 * width, t_ref, H_C, None)
        attend_block(image_ref, text_ref, text_ref, 0, width, 2 * width, i_ref, H_C, len_ref[0])

    flops = 8 * text.shape[0] * image.shape[0] * width * 8
    outs = [(text.shape[0], width), (image.shape[0], width)]
    return vmem_call(body, 2, outs, length, flops, text, image)


def cross_attend_back(text, image, length, t_grad, i_grad):
    width = text.shape[1] // 3

    def body(len_ref, text_ref, image_ref, tg_ref, ig_ref, dt_ref, di_ref):
        attend_block_back(
            text_ref, image_ref, image_ref, 0, width, 2 * width, tg_ref, dt_ref, di_ref, di_ref, H_C, None
        )
        attend_block_back(
            image_ref, text_ref, text_ref, 0, width, 2 * width, ig_ref, di_ref, dt_ref, dt_ref, H_C, len_ref[0]
        )

    flops = 20 * text.shape[0] * image.shape[0] * width * 8
    return vmem_call(body, 4, [text.shape, image.shape], length, flops, text, image, t_grad, i_grad)


def self_attend(packed, heads, length, masked):
    width = packed.shape[1] // 3

    def body(len_ref, ref, out_ref):
        attend_block(ref, ref, ref, 0, width, 2 * width, out_ref, heads, len_ref[0] if masked else None)

    flops = 4 * packed.shape[0] * packed.shape[0] * width * 8
    return vmem_call(body, 1, [(packed.shape[0], width)], length, flops, packed)[0]


def self_attend_back(packed, heads, length, masked, grad):
    width = packed.shape[1] // 3

    def body(len_ref, ref, g_ref, d_ref):
        attend_block_back(
            ref, ref, ref, 0, width, 2 * width, g_ref, d_ref, d_ref, d_ref, heads, len_ref[0] if masked else None
        )

    flops = 10 * packed.shape[0] * packed.shape[0] * width * 8
    return vmem_call(body, 2, [packed.shape], length, flops, packed, grad)[0]


def tail_forward(residual, attn_low, out_mat, up_mat, down_mat, gain_pair):
    first_sum = residual + mm(attn_low, out_mat)
    first_norm = layer_norm(first_sum, gain_pair[0])
    hidden_low = first_norm.astype(BFLOAT)
    upper = mm(hidden_low, up_mat)
    active = jax.nn.gelu(upper).astype(BFLOAT)
    second_sum = first_norm + mm(active, down_mat)
    return layer_norm(second_sum, gain_pair[1]), (first_sum, hidden_low, upper, active, second_sum)


def tail_backward(grad_result, kept, attn_low, out_mat, up_mat, down_mat, gain_pair, down_natural):
    first_sum, hidden_low, upper, active, second_sum = kept
    grad_second, gain_two = norm_back(second_sum, gain_pair[1], grad_result)
    low = grad_second.astype(BFLOAT)
    grad_down = whole_item(active, low) if down_natural else whole_item(low, active)
    grad_upper = gelu_back(upper, mm_t(low, down_mat)).astype(BFLOAT)
    grad_up = whole_item(grad_upper, hidden_low)
    grad_norm = grad_second + mm_t(grad_upper, up_mat)
    grad_first, gain_one = norm_back(first_sum, gain_pair[0], grad_norm)
    grad_first_low = grad_first.astype(BFLOAT)
    grad_out = whole_item(attn_low, grad_first_low)
    grad_attn = mm_t(grad_first_low, out_mat).astype(BFLOAT)
    return grad_first, grad_attn, [grad_down, grad_up, grad_out], [gain_one, gain_two]


def project(stream_low, proj):
    return mm(stream_low, proj).astype(BFLOAT)


def whole_item(rows, other):
    return (rows, 0, rows.shape[1], other)


def third_items(packed, other):
    span = packed.shape[1] // 3
    return [(packed, e * span, span, other) for e in range(3)]


def side(shards):
    return jnp.concatenate(shards, axis=1)


def on_device(
    text_input,
    image_input,
    caption_lengths,
    text_cotangent,
    image_cotangent,
    cross_text_proj,
    cross_image_proj,
    cross_text_out,
    cross_image_out,
    cross_text_up,
    cross_text_down,
    cross_image_up,
    cross_image_down,
    self_text_proj,
    self_text_out,
    self_text_up,
    self_text_down,
    self_image_proj,
    self_image_out,
    self_image_up,
    self_image_down,
    text_gains,
    image_gains,
):
    d_t = text_input.shape[2]
    d_v = image_input.shape[2]
    co = cross_text_proj.shape[2]
    ff_t = cross_text_up.shape[1]
    n_text = text_input.shape[1]

    size = lax.axis_size("dp") * lax.axis_size("seq")
    bits = sum(device_bits())
    by_permute = size == 1 << bits and all(
        m.shape[-2] % 8 == 0 for m in (cross_text_out, cross_text_down, self_text_down)
    )

    def gather_columns(parts):
        return lax.all_gather(side(parts), ALL, axis=0, tiled=True)

    own_t, own_v = d_t // size, d_v // size
    own_f, own_c = ff_t // size, co // size
    text_parts = list(cross_text_proj) + [cross_text_up] + list(self_text_proj)
    text_wide = gather_columns(text_parts + [self_text_out, self_text_up])
    image_parts = [cross_image_out, cross_image_up, cross_image_down] + list(self_image_proj)
    image_wide = gather_columns(image_parts + [self_image_out, self_image_up, self_image_down])
    w_ctp = text_wide[:, : 3 * co]

    high = list(range(3, bits))[::-1]
    x_first = high + [2, 0, 1]
    y_first = high + [0, 2, 1]
    shards = [
        (side(list(cross_image_proj)), y_first, None),
        (jnp.concatenate([cross_text_down, cross_text_out], axis=0), x_first, [own_f, own_c]),
        (self_text_down, x_first, None),
    ]

    panel = 128
    my_len = lax.dynamic_index_in_dim(caption_lengths, lax.axis_index("seq"), 0, keepdims=True)
    x_t = text_input[0]
    x_v = image_input[0]

    if by_permute:
        movers = [Gather(*item) for item in shards]
        for turn_at in range(bits):
            active = movers[:2] + ([movers[2]] if turn_at >= 2 else [])
            for m in active:
                m.start()
            close_round(active)
        w_cip = movers[0].full[0]
        w_ctd, w_cto = movers[1].full
        movers[2].start()
        t_packed = project(x_t, w_ctp)
        i_packed = project(x_v, w_cip)
        t_attn, i_attn = cross_attend(t_packed, i_packed, my_len)
        t_attn, i_attn = close_round(movers[2:], t_attn, i_attn)
        movers[2].start()
    else:
        full = [lax.all_gather(shard, ALL, axis=0) for shard, order, splits in shards]
        w_ctd, w_cto = full[1][:, :own_f], full[1][:, own_f:]
        w_cip, w_ctd, w_cto, w_std = (w.reshape(-1, w.shape[-1]) for w in (full[0], w_ctd, w_cto, full[2]))
        t_packed = project(x_t, w_ctp)
        i_packed = project(x_v, w_cip)
        t_attn, i_attn = cross_attend(t_packed, i_packed, my_len)

    w_ctu = text_wide[:, 3 * co : 3 * co + ff_t]
    text_self = text_wide[:, 3 * co + ff_t :]
    w_stp, w_sto, w_stu = text_self[:, : 3 * d_t], text_self[:, 3 * d_t : 4 * d_t], text_self[:, 4 * d_t :]

    def halving(*picks):
        return [1] + list(picks) + [b for b in range(bits) if b != 1 and b not in picks]

    t_cross, t_kept = tail_forward(x_t.astype(FLOAT), t_attn, w_cto, w_ctu, w_ctd, text_gains[0:2])
    t_low = t_cross.astype(BFLOAT)
    if by_permute:
        t_cross, t_kept = close_round(movers[2:], t_cross, t_kept)
        w_std = movers[2].full[0]
        t_low = t_cross.astype(BFLOAT)
    st_packed = project(t_low, w_stp)
    st_attn = self_attend(st_packed, H_T, my_len, True)
    t_final, st_kept = tail_forward(t_cross, st_attn, w_sto, w_stu, w_std, text_gains[2:4])
    t_res, t_ga, t_pairs, t_gain_s = tail_backward(
        text_cotangent[0].astype(FLOAT), st_kept, st_attn, w_sto, w_stu, w_std, text_gains[2:4], False
    )
    def start(*movers):
        for m in movers:
            if m.step < bits:
                m.start()

    def by_owner(packed, own):
        rows = packed.shape[0]
        blocks = packed.reshape(rows, 3, size, own).transpose(2, 0, 1, 3).reshape(size, rows, 3 * own)
        return jnp.pad(blocks, ((0, 0), (0, -rows % 8), (0, 3 * (own_v - own))))

    def exchange(*blocks):
        return lax.all_to_all(
            jnp.concatenate(blocks, axis=1), ALL, split_axis=0, concat_axis=0, tiled=True
        )

    c1a = Chunk(t_pairs[:1], d_t, halving(2, 0))
    c1b = Chunk(t_pairs[1:], d_t, halving(0, 2))
    t_ga, t_res, i_attn = close_round([], t_ga, t_res, i_attn)

    start(c1a, c1b)
    st_grads = self_attend_back(st_packed, H_T, my_len, True, t_ga)
    t_back = t_res + mm_t(st_grads, w_stp)
    st_grads, t_back, i_attn = close_round([c1a, c1b], st_grads, t_back, i_attn)

    start(c1a, c1b)
    t_res, t_ga, t_pairs, t_gain_c = tail_backward(
        t_back, t_kept, t_attn, w_cto, w_ctu, w_ctd, text_gains[0:2], True
    )
    c3a = Chunk([t_pairs[0], t_pairs[2]], d_t, halving(2, 0))
    c3b = Chunk(t_pairs[1:2], d_t, halving(0, 2))
    c3a.send, c3a.keep, c3b.send, c3b.keep, t_res, t_ga, i_attn = close_round(
        [c1a, c1b], c3a.send, c3a.keep, c3b.send, c3b.keep, t_res, t_ga, i_attn
    )
    start(c1a, c1b, c3a, c3b)
    (i_attn,) = close_round([c1a, c1b, c3a, c3b], i_attn)

    w_cio, w_ciu, w_cid = (image_wide[:, i * d_v : (i + 1) * d_v] for i in range(3))
    w_sip = image_wide[:, 3 * d_v : 6 * d_v]
    w_sio, w_siu, w_sid = (image_wide[:, (6 + i) * d_v : (7 + i) * d_v] for i in range(3))

    start(c3a, c3b, c1a, c1b)
    i_cross, i_kept = tail_forward(x_v.astype(FLOAT), i_attn, w_cio, w_ciu, w_cid, image_gains[0:2])
    i_low = i_cross.astype(BFLOAT)
    if by_permute:
        tall = -(-x_t.shape[0] // 8) * 8
        seen = [x_v.reshape(-1, d_t), i_low.reshape(-1, d_t)]
        seen += [jnp.pad(m, ((0, tall - m.shape[0]), (0, 0))) for m in (x_t, t_low)]
        seen = jnp.concatenate(seen, axis=0)
    si_packed = project(i_low, w_sip)
    si_attn = self_attend(si_packed, H_V, my_len, False)
    i_final, si_kept = tail_forward(i_cross, si_attn, w_sio, w_siu, w_sid, image_gains[2:4])
    i_res, i_ga, i_pairs, i_gain_s = tail_backward(
        image_cotangent[0].astype(FLOAT), si_kept, si_attn, w_sio, w_siu, w_sid, image_gains[2:4], False
    )
    c1i = Chunk(i_pairs, d_v, halving(0, 2))
    c1i.send, c1i.keep, i_ga, i_res = close_round(
        [c1a, c1b, c3a, c3b], c1i.send, c1i.keep, i_ga, i_res
    )
    if by_permute:
        seen = lax.all_gather(seen, ALL, axis=0)

    start(c1i, c3a, c3b)
    si_grads = self_attend_back(si_packed, H_V, my_len, False, i_ga)
    i_back = i_res + mm_t(si_grads, w_sip)
    si_grads, i_back = close_round([c1i, c3a, c3b], si_grads, i_back)
    self_slices = t_low
    if by_permute:
        self_slices = exchange(by_owner(st_grads, own_t), by_owner(si_grads, own_v))

    start(c1i, c3a, c3b)
    i_res, i_ga, i_pairs, i_gain_c = tail_backward(
        i_back, i_kept, i_attn, w_cio, w_ciu, w_cid, image_gains[0:2], True
    )
    c3x = Chunk(i_pairs[:1], d_v, halving(2, 0))
    c3y = Chunk(i_pairs[1:], d_v, halving(0, 2))
    c3x.send, c3x.keep, c3y.send, c3y.keep, i_res, i_ga, t_ga = close_round(
        [c1i, c3a, c3b], c3x.send, c3x.keep, c3y.send, c3y.keep, i_res, i_ga, t_ga
    )

    start(c3x, c3y, c1i)
    t_grads, i_grads = cross_attend_back(t_packed, i_packed, my_len, t_ga, i_ga)
    t_grads, i_grads = close_round([c3x, c3y, c1i], t_grads, i_grads)

    t_gain = jnp.stack(t_gain_c + t_gain_s)
    i_gain = jnp.stack(i_gain_c + i_gain_s)
    start(c3x, c3y, c1i)
    if by_permute:
        gain_rows = [t_gain.reshape(4, size, own_t), i_gain.reshape(4, size, own_v)]
        gain_rows = [
            jnp.pad(g.astype(BFLOAT), ((0, 0), (0, 0), (0, 3 * own_v - g.shape[2]))) for g in gain_rows
        ]
        gain_rows = jnp.concatenate(gain_rows, axis=0).transpose(1, 0, 2)
        cross_slices = exchange(by_owner(t_grads, own_c), by_owner(i_grads, own_c), gain_rows)
    close_round([c3x, c3y, c1i])
    start(c3x, c3y, c1i)
    text_input_grad = t_res + mm_t(t_grads, w_ctp)
    image_input_grad = i_res + mm_t(i_grads, w_cip)
    rows_all = t_low
    if by_permute:
        short = x_v.size // d_t
        wide_v = x_v.shape[0]
        tall_v = -(-wide_v // 8) * 8
        rows_all = (
            seen[:, :short].reshape(-1, d_v),
            seen[:, short : 2 * short].reshape(-1, d_v),
            seen[:, 2 * short : 2 * short + tall].reshape(-1, d_t),
            seen[:, 2 * short + tall :].reshape(-1, d_t),
        )
    text_input_grad, image_input_grad, rows_all = close_round(
        [c3x, c3y, c1i], text_input_grad, image_input_grad, rows_all
    )

    def slices_grad(rows, part, own):
        grad = t_mm(rows, part.reshape(-1, part.shape[2]))[:, : 3 * own]
        return grad.reshape(grad.shape[0], 3, own).transpose(1, 0, 2)

    start(c3x, c3y, c3a, c3b)
    self_grads, cross_grads = t_low, t_low
    if by_permute:
        all_v, all_low_v, all_t, all_low_t = rows_all
        self_grads = (
            slices_grad(all_low_t, self_slices[:, :tall], own_t),
            slices_grad(all_low_v, self_slices[:, tall : tall + wide_v], own_v),
        )
    (self_grads,) = close_round([c3x, c3y, c3a, c3b], self_grads)
    start(c3x, c3y, c1a, c1b)
    if by_permute:
        cross_grads = (
            slices_grad(all_t, cross_slices[:, :tall], own_c),
            slices_grad(all_v, cross_slices[:, tall : tall + wide_v], own_c),
            jnp.sum(cross_slices[:, tall + tall_v :].astype(FLOAT), axis=0),
        )
    (cross_grads,) = close_round([c3x, c3y, c1a, c1b], cross_grads)
    for m in (c1a, c1b, c3a, c3b, c1i, c3x, c3y):
        while m.step < bits:
            m.start()
            m.absorb()

    if by_permute:
        o_stp, o_sip = self_grads
        o_ctp, o_cip, gain_sum = cross_grads
        o_tg, o_ig = gain_sum[:4, :own_t], gain_sum[4:, :own_v]
    else:

        def by_scatter(packed, rows):
            whole = Whole(third_items(packed, rows), rows.shape[1])
            whole.launch()
            block = whole.finish()
            return block.reshape(3, block.shape[0] // 3, block.shape[1]).transpose(0, 2, 1)

        o_stp, o_sip = by_scatter(st_grads, t_low), by_scatter(si_grads, i_low)
        o_ctp, o_cip = by_scatter(t_grads, x_t), by_scatter(i_grads, x_v)
        at = my_index()
        t_gain, i_gain = lax.psum(t_gain, ALL), lax.psum(i_gain, ALL)
        o_tg = lax.dynamic_slice_in_dim(t_gain, at * own_t, own_t, 1)
        o_ig = lax.dynamic_slice_in_dim(i_gain, at * own_v, own_v, 1)

    def cut(block, rows):
        out, at = [], 0
        for r in rows:
            out.append(block[at : at + r])
            at += r
        return out

    (g_std,) = cut(c1a.full, (ff_t // d_t * own_t,))
    g_stu, g_sto = cut(c1b.full, (own_f, own_t))
    g_sid, g_siu, g_sio = cut(c1i.full, (own_v,) * 3)
    g_ctd, g_cto = cut(c3a.full, (own_f, own_c))
    g_ctu, g_cid = c3b.full, c3x.full
    g_ciu, g_cio = cut(c3y.full, (own_v,) * 2)
    g_std = g_std.reshape(ff_t // d_t, own_t, d_t).transpose(1, 0, 2).reshape(own_t, ff_t)

    o_stu, o_ctu, o_ctd = g_stu.T, g_ctu.T, g_ctd
    o_std, o_sto = g_std.T, g_sto
    o_sid, o_siu, o_sio = g_sid.T, g_siu.T, g_sio
    o_cid, o_ciu, o_cio, o_cto = g_cid, g_ciu.T, g_cio, g_cto
    return (
        t_final.astype(BFLOAT)[None],
        i_final.astype(BFLOAT)[None],
        text_input_grad[None],
        image_input_grad[None],
        o_ctp,
        o_cip,
        o_cto,
        o_cio,
        o_ctu,
        o_ctd,
        o_ciu,
        o_cid,
        o_stp,
        o_sto,
        o_stu,
        o_std,
        o_sip,
        o_sio,
        o_siu,
        o_sid,
        o_tg,
        o_ig,
    )


def solution(mesh):
    row = P(ALL, None)
    batch = P(ALL, None, None)
    col = P(None, ALL)
    proj = P(None, ALL, None)
    proj_grad = P(None, None, ALL)
    in_specs = (batch, batch, P("dp"), batch, batch, proj, proj, row, row, row, row, row, row)
    in_specs += (proj, row, row, row, proj, row, row, row, P(), P())
    out_specs = (batch, batch, batch, batch, proj_grad, proj_grad, row, row, col, row, col, row)
    out_specs += (proj_grad, row, col, col, proj_grad, row, col, col, col, col)
    return jax.shard_map(
        on_device, mesh=mesh, in_specs=in_specs, out_specs=out_specs, check_vma=False
    )
```
